32 devices in a mesh: freq: 2 (over y), row: 4 (over z), col: 2 (over x), cplx: 2 (over core).
Axes of the slice: x: 2, y: 2, z: 4, core: 2. Of those that a mesh axis runs over, the one named last changes fastest.
Arguments:
- u_bases: bfloat16 [8, 8, 2, 128, 512], P(('freq', 'row'), ('col', 'cplx')), parts along dimension 0
- v_bases: bfloat16 [8, 8, 2, 128, 512], P(('freq', 'row'), ('col', 'cplx')), parts along dimension 0
- tile_ranks: int32 [8, 8], P(('freq', 'row'), ('col', 'cplx')), parts along dimension 0, may hold values from 32 to 128, as said below
- u_unit: float32 [64, 2, 2048], P(('freq', 'col', 'cplx'), None, 'row'), parts along dimension 0, may hold values from -6 to 6
- v_unit: float32 [64, 2, 4096], P(('freq', 'row'), None, ('col', 'cplx')), parts along dimension 0, may hold values from -6 to 6
- x_solution: float32 [64, 2, 4096], P(('freq', 'row'), None, ('col', 'cplx')), parts along dimension 0, may hold values from -6 to 6
- w_direction: float32 [64, 2, 4096], P(('freq', 'row'), None, ('col', 'cplx')), parts along dimension 0, may hold values from -6 to 6
- alpha_prev: float32 [64], P('freq'), parts along dimension 0, may hold values from 0.5 to 2
- rhobar_prev: float32 [64], P('freq'), parts along dimension 0, may hold values from 0.5 to 2
- phibar_prev: float32 [64], P('freq'), parts along dimension 0, may hold values from 0.5 to 2
Outputs:
- x_next: float32 [64, 2, 4096], P(('freq', 'row'), None, ('col', 'cplx')), parts along dimension 0
- w_next: float32 [64, 2, 4096], P(('freq', 'row'), None, ('col', 'cplx')), parts along dimension 0
- u_next: float32 [64, 2, 2048], P(('freq', 'col', 'cplx'), None, 'row'), parts along dimension 0
- v_next: float32 [64, 2, 4096], P(('freq', 'row'), None, ('col', 'cplx')), parts along dimension 0
- alpha_next: float32 [64], P('freq'), parts along dimension 0
- rhobar_next: float32 [64], P('freq'), parts along dimension 0
- phibar_next: float32 [64], P('freq'), parts along dimension 0
The draws below stay inside these ranges and needn't reach their ends.
There are 2 independent parts, one for each index of `freq`. The reference program is written for one: setup_inputs(seed, part) draws one part's arguments, and reference() takes and returns one part's arrays. A program takes and returns all parts, laid end to end along the dimension named above; each array names one. Nothing has to cross between parts.
Inputs may be any that keep to these rules, and one draw needn't show every extreme that they name: `tile_ranks`: some tile has rank 128.
All inputs are finite; a program needn't handle non-finite values.
Results may differ from the reference program's by a relative error of at most 0.011.
Values may be sent and summed in bfloat16 or wider, within the bound.
No kernel may reach another device: no remote copies, remote signals or barrier semaphores. Data moves between devices by JAX's collectives and lax.ppermute only.
A program may use at most 64 MiB of HBM per device.

```python
import math
import jax
import jax.numpy as jnp
from jax import lax

TILE = 512
RMAX = 128
RT = 1
CT = 2
MT = 4
NT = 8
M = 2048
N = 4096
NV = 32
N_ROW = 4
N_COL = 2
N_CPLX = 2


def scaled_bases(entries, key, along, fan):
    extent = entries.shape[along]
    ladder = jnp.arange(extent, dtype=jnp.float32) / max(extent - 1, 1)
    factor = 10.0 ** (ladder - 0.5)
    layout = [1, 1, 1, 1, 1]
    layout[along] = extent
    tile_gain = jax.random.uniform(key, (entries.shape[0], entries.shape[1], 1, 1, 1), jnp.float32, 0.7, 1.4)
    return (entries * factor.reshape(layout) * tile_gain / math.sqrt(fan)).astype(jnp.bfloat16)


def draw_u_bases(key, part):
    key = jax.random.fold_in(key, 1)
    keys = jax.random.split(key, 2)
    layout = (MT, NT, 2, RMAX, TILE)
    entries = jax.random.normal(keys[0], layout, jnp.float32)
    return scaled_bases(entries, keys[1], 0, 2 * RMAX)


def draw_v_bases(key, part):
    key = jax.random.fold_in(key, 2)
    keys = jax.random.split(key, 2)
    layout = (MT, NT, 2, RMAX, TILE)
    entries = jax.random.normal(keys[0], layout, jnp.float32)
    return scaled_bases(entries, keys[1], 1, 2 * TILE * NT)


def draw_tile_ranks(key, part):
    key = jax.random.fold_in(key, 3)
    keys = jax.random.split(key, 2)
    values = jax.random.randint(keys[0], (MT, NT), RMAX // 4, RMAX + 1)
    chosen = jax.random.randint(keys[1], (), 0, MT * NT)
    position = jnp.arange(MT * NT).reshape(MT, NT)
    return jnp.where(position == chosen, RMAX, values).astype(jnp.int32)


def block_levels(stream_key, shape, shards, smallest, high):
    def one(dim, blocks):
        steps = jax.random.uniform(jax.random.fold_in(jax.random.fold_in(stream_key, 6), dim), (blocks,), jnp.float32, smallest / len(shards), high / len(shards))
        return jnp.repeat(jnp.exp(steps), shape[dim] // blocks).reshape((-1,) + (1,) * (len(shape) - dim - 1))

    factor_of = one(*shards[0])
    for cut in shards[1:]:
        factor_of = factor_of * one(*cut)
    return factor_of


def gaussian(rng, dims, scale, most, cuts=(), kind=jnp.bfloat16):
    array = jax.random.normal(rng, dims, jnp.float32) * scale
    if len(cuts) > 0:
        array = block_levels(rng, dims, cuts, -0.22, 0.18) * array
    return jnp.clip(array, min=-most, max=most).astype(kind)


def setup_inputs(seed: int = 0, part: int = 0) -> dict:
    arg_keys = jax.random.split(jax.random.key(seed), 11)
    part_keys = jax.random.split(jax.random.fold_in(arg_keys[10], part), 11)
    return {
        "u_bases": draw_u_bases(jax.random.fold_in(jax.random.fold_in(arg_keys[10], part), 71), part),
        "v_bases": draw_v_bases(jax.random.fold_in(jax.random.fold_in(arg_keys[10], part), 71), part),
        "tile_ranks": draw_tile_ranks(jax.random.fold_in(jax.random.fold_in(arg_keys[10], part), 71), part),
        "u_unit": gaussian(part_keys[3], (NV, 2, M), 1.0, 6.0, ((0, 4), (2, 4)), jnp.float32),
        "v_unit": gaussian(part_keys[4], (NV, 2, N), 1.0, 6.0, ((0, 4), (2, 4)), jnp.float32),
        "x_solution": gaussian(part_keys[5], (NV, 2, N), 1.0, 6.0, ((0, 4), (2, 4)), jnp.float32),
        "w_direction": gaussian(part_keys[6], (NV, 2, N), 1.0, 6.0, ((0, 4), (2, 4)), jnp.float32),
        "alpha_prev": jnp.clip(jax.random.uniform(part_keys[7], (NV,), jnp.float32, 0.5, 2.0), 0.5, 2.0),
        "rhobar_prev": jnp.clip(jax.random.uniform(part_keys[8], (NV,), jnp.float32, 0.5, 2.0), 0.5, 2.0),
        "phibar_prev": jnp.clip(jax.random.uniform(part_keys[9], (NV,), jnp.float32, 0.5, 2.0), 0.5, 2.0),
    }


epsilon = 1e-06

def rounded(value):
    return lax.optimization_barrier(value.astype(jnp.bfloat16)).astype(jnp.float32)

def product(form, first, second):
    return jnp.einsum(form, first.astype(jnp.float32), second.astype(jnp.float32))

def reference(u_bases, v_bases, tile_ranks, u_unit, v_unit, x_solution, w_direction, alpha_prev, rhobar_prev, phibar_prev):
    group_cols = N_COL * N_CPLX
    rank_live = (jnp.arange(RMAX, dtype=jnp.int32)[None, None, :] < tile_ranks[:, :, None]).astype(jnp.float32)
    model_low = rounded(v_unit).reshape(NV, 2, NT, TILE)

    def forward_row(row_index):
        left = u_bases[row_index].astype(jnp.float32)
        right = v_bases[row_index].astype(jnp.float32)
        coef_re = product('qri,nqi->nqr', right[:, 0], model_low[:, 0]) + product('qri,nqi->nqr', right[:, 1], model_low[:, 1])
        coef_im = product('qri,nqi->nqr', right[:, 0], model_low[:, 1]) - product('qri,nqi->nqr', right[:, 1], model_low[:, 0])
        mask_row = rank_live[row_index][None]
        coef_re = rounded(coef_re * mask_row)
        coef_im = rounded(coef_im * mask_row)
        out_re = product('qri,nqr->nqi', left[:, 0], coef_re) - product('qri,nqr->nqi', left[:, 1], coef_im)
        out_im = product('qri,nqr->nqi', left[:, 0], coef_im) + product('qri,nqr->nqi', left[:, 1], coef_re)
        stacked = jnp.stack([out_re, out_im], 1)
        grouped = rounded(stacked.reshape(NV, 2, group_cols, CT, TILE).sum(3))
        return grouped.sum(2)
    forward = lax.map(forward_row, jnp.arange(MT))
    forward = jnp.transpose(forward, (1, 2, 0, 3)).reshape(NV, 2, M)
    residual_u = forward - alpha_prev[:, None, None] * u_unit
    beta_all = jnp.sqrt(lax.optimization_barrier(jnp.mean(residual_u * residual_u, axis=(1, 2))) + epsilon)
    u_next = residual_u / beta_all[:, None, None]
    unit_low = rounded(u_next).reshape(NV, 2, MT, TILE)

    def adjoint_col(col_index):
        left = u_bases[:, col_index].astype(jnp.float32)
        right = v_bases[:, col_index].astype(jnp.float32)
        coef_re = product('pri,npi->npr', left[:, 0], unit_low[:, 0]) + product('pri,npi->npr', left[:, 1], unit_low[:, 1])
        coef_im = product('pri,npi->npr', left[:, 0], unit_low[:, 1]) - product('pri,npi->npr', left[:, 1], unit_low[:, 0])
        mask_col = rank_live[:, col_index][None]
        coef_re = rounded(coef_re * mask_col)
        coef_im = rounded(coef_im * mask_col)
        out_re = product('pri,npr->npi', right[:, 0], coef_re) - product('pri,npr->npi', right[:, 1], coef_im)
        out_im = product('pri,npr->npi', right[:, 0], coef_im) + product('pri,npr->npi', right[:, 1], coef_re)
        stacked = jnp.stack([out_re, out_im], 1)
        grouped = rounded(stacked.reshape(NV, 2, N_ROW, RT, TILE).sum(3))
        return grouped.sum(2)
    back = lax.map(adjoint_col, jnp.arange(NT))
    back = jnp.transpose(back, (1, 2, 0, 3)).reshape(NV, 2, N)
    residual_v = M / N * back - beta_all[:, None, None] * v_unit
    alpha_next = jnp.sqrt(lax.optimization_barrier(jnp.mean(residual_v * residual_v, axis=(1, 2))) + epsilon)
    v_next = residual_v / alpha_next[:, None, None]
    rho_all = jnp.sqrt(rhobar_prev * rhobar_prev + beta_all * beta_all)
    cosine = rhobar_prev / rho_all
    sine = beta_all / rho_all
    theta = sine * alpha_next
    rhobar_next = -cosine * alpha_next
    phi_all = cosine * phibar_prev
    phibar_next = sine * phibar_prev
    x_next = x_solution + (phi_all / rho_all)[:, None, None] * w_direction
    w_next = v_next - (theta / rho_all)[:, None, None] * w_direction
    return (x_next, w_next, u_next, v_next, alpha_next, rhobar_next, phibar_next)
```

```python
from functools import partial

import jax
import jax.numpy as jnp
from jax import lax
from jax.experimental import pallas as pl
from jax.experimental.pallas import tpu as pltpu
from jax.sharding import PartitionSpec as P

epsilon = 1e-06
shrink = 2.0**-20
f32 = jnp.float32
bf16 = jnp.bfloat16


def call(kernel, outs, *args, scratch=()):
    in_specs = [
        pl.BlockSpec(memory_space=pltpu.SMEM if a.dtype == jnp.int32 else pltpu.VMEM) for a in args
    ]
    return pl.pallas_call(
        kernel,
        out_shape=[jax.ShapeDtypeStruct(s, d) for s, d in outs],
        in_specs=in_specs,
        out_specs=[pl.BlockSpec(memory_space=pltpu.VMEM)] * len(outs),
        scratch_shapes=list(scratch),
        compiler_params=pltpu.CompilerParams(vmem_limit_bytes=40 * 2**20),
    )(*args)


def iota(shape, dim):
    return lax.broadcasted_iota(jnp.int32, shape, dim)


def to_lanes(column, place, lanes):
    rows = column.shape[0]
    here = iota((rows, lanes), 1) == place
    return jnp.sum(jnp.where(here, column, 0.0), axis=0, keepdims=True)


def to_column(lane_values, first, rows):
    lanes = lane_values.shape[1]
    here = iota((rows, lanes), 1) == iota((rows, lanes), 0) + first
    return jnp.sum(jnp.where(here, lane_values, 0.0), axis=1, keepdims=True)


def dot(a, b, transposed):
    return lax.dot_general(a, b, (((1,), (1 if transposed else 0,)), ((), ())), preferred_element_type=f32)


def through(inner, outer, ranks_ref, x, own):
    total = []
    tiles, _, ranks, size = inner.shape[1:]
    for q in range(tiles):
        g = dot(x(q), inner[0, q].reshape(2 * ranks, size), True)
        rows = g.shape[0]
        g = g.reshape(rows // (2 * own), 2, own, 2 * ranks)
        live = iota((1, 1, ranks), 2) < ranks_ref[0, q]
        re = jnp.where(live, g[:, 0, :, :ranks] + g[:, 1, :, ranks:], 0.0)
        im = jnp.where(live, g[:, 1, :, :ranks] - g[:, 0, :, ranks:], 0.0)
        both = jnp.stack([jnp.concatenate([re, -im], 2), jnp.concatenate([im, re], 2)], 1)
        both = both.reshape(rows, 2 * ranks).astype(bf16)
        total.append(dot(both, outer[0, q].reshape(2 * ranks, size), False))
    return total


def pack_kernel(v_ref, out_ref):
    own = v_ref.shape[0]
    out_ref[...] = jnp.concatenate([v_ref[:, 0, :], v_ref[:, 1, :]], 0).astype(bf16)


def forward_kernel(n_row, own_v, own_u, where_ref, ranks_ref, u_bases, v_bases, u_ref, alpha_ref, *refs):
    blocks, (low_ref, own_ref, total) = refs[:n_row], refs[n_row:]
    p, c = where_ref[0], where_ref[1]
    size = v_bases.shape[4]
    x = jnp.concatenate([b[...] for b in blocks], 0)
    parts = through(v_bases, u_bases, ranks_ref, lambda q: x[:, q * size : (q + 1) * size], own_v)
    total[...] = sum(parts[1:], parts[0])
    many = own_u // own_v
    for b in range(many):
        at = pl.ds(pl.multiple_of(((c * many + b) ^ p) * 2 * own_v, 2 * own_v), 2 * own_v)
        alpha = to_column(alpha_ref[...], c * own_u + b * own_v, own_v)
        mine = slice(b * own_v, (b + 1) * own_v)
        shift = jnp.concatenate([alpha * u_ref[mine, 0, :], alpha * u_ref[mine, 1, :]], 0)
        left = total[at, :] - shift
        own_ref[b * 2 * own_v : (b + 1) * 2 * own_v, :] = left
        total[at, :] = left
    low_ref[...] = total[...].astype(bf16)


def adjoint_kernel(n_row, n_got, own_v, own_u, lanes, where_ref, ranks_ref, u_bases, v_bases, own_ref, sum_ref, *refs):
    got, outs, own_out, total = refs[:n_got], refs[n_got : n_got + n_row], refs[n_got + n_row], refs[-1]
    p, c = where_ref[0], where_ref[1]
    many = own_u // own_v
    for b in range(many):
        at = pl.ds(pl.multiple_of(((c * many + b) ^ p) * 2 * own_v, 2 * own_v), 2 * own_v)
        mine = slice(b * 2 * own_v, (b + 1) * 2 * own_v)
        acc = own_ref[mine, :]
        for g in got:
            acc = acc + g[at, :].astype(f32)
        own_out[mine, :] = acc
    res = sum_ref[...].astype(f32) + got[-1][...].astype(f32)
    rows = res.shape[0]
    squares = jnp.sum(res * res, axis=1, keepdims=True)
    row = iota((rows, 1), 0)
    place = ((row // (2 * own_v)) ^ p) * own_v + row % own_v
    beta2 = to_lanes(squares, place, lanes)
    high = beta2.astype(bf16)
    low = (beta2 - high.astype(f32)).astype(bf16)
    tail = jnp.where(iota((2 * own_v, lanes), 0) == 0, high.astype(f32), low.astype(f32)).astype(bf16)
    x = (res * shrink).astype(bf16)
    parts = through(u_bases, v_bases, ranks_ref, lambda q: x, own_v)
    wide = parts[0].shape[1]
    for k, out in enumerate(outs):
        for q, part in enumerate(parts):
            out[:, q * wide : (q + 1) * wide] = part[k * 2 * own_v : (k + 1) * 2 * own_v].astype(bf16)
        out[:, len(parts) * wide :] = tail


def pairs(values):
    while len(values) > 1:
        values = [a + b for a, b in zip(values[::2], values[1::2])]
    return values[0]


def residual_kernel(n_row, rows_total, cols_total, lanes, where_ref, v_ref, *refs):
    blocks, (res_ref, beta_ref, norm_ref) = refs[:n_row], refs[n_row:]
    p = where_ref[0]
    own_v, _, wide = v_ref.shape
    beta2 = pairs([b[0:1, wide:].astype(f32) + b[1:2, wide:].astype(f32) for b in blocks])
    beta = jnp.sqrt(beta2 / (2 * rows_total) + epsilon)
    beta_ref[...] = beta
    mine = to_column(beta, p * own_v, own_v)
    scale = rows_total / cols_total / shrink / mine
    squares = None
    for i in range(2):
        half = slice(i * own_v, (i + 1) * own_v)
        back = pairs([b[half, :wide].astype(f32) for b in blocks])
        res = scale * back - mine * v_ref[:, i, :]
        res_ref[half, :] = res
        here = jnp.sum(res * res, axis=1, keepdims=True)
        squares = here if squares is None else squares + here
    place = iota((own_v, 1), 0) + p * own_v
    norm_ref[...] = jnp.broadcast_to(to_lanes(squares, place, lanes), norm_ref.shape)


def update_kernel(
    cols_total,
    where_ref,
    norms_ref,
    beta_ref,
    res_ref,
    own_ref,
    x_ref,
    w_ref,
    rhobar_ref,
    phibar_ref,
    x_out,
    w_out,
    u_out,
    v_out,
    alpha_out,
    rhobar_out,
    phibar_out,
):
    p, c = where_ref[0], where_ref[1]
    own_v = x_ref.shape[0]
    own_u = u_out.shape[0]
    many = own_u // own_v
    rhs = alpha_out.shape[1]
    beta = beta_ref[:, :rhs]
    rhobar, phibar = rhobar_ref[...], phibar_ref[...]
    alpha2 = jnp.sum(norms_ref[...], axis=0, keepdims=True)[:, :rhs]
    alpha = jnp.sqrt(alpha2 / (2 * cols_total) + epsilon)
    rho = jnp.sqrt(rhobar * rhobar + beta * beta)
    cosine = rhobar / rho
    sine = beta / rho
    alpha_out[...] = alpha
    rhobar_out[...] = -cosine * alpha
    phibar_out[...] = sine * phibar
    step_x = to_column(cosine * phibar / rho, p * own_v, own_v)
    step_w = to_column(sine * alpha / rho, p * own_v, own_v)
    alpha_own = to_column(alpha, p * own_v, own_v)
    for i in range(2):
        w = w_ref[:, i, :]
        v = res_ref[i * own_v : (i + 1) * own_v, :] / alpha_own
        x_out[:, i, :] = x_ref[:, i, :] + step_x * w
        v_out[:, i, :] = v
        w_out[:, i, :] = v - step_w * w
    for b in range(many):
        beta_own = to_column(beta, c * own_u + b * own_v, own_v)
        for i in range(2):
            u = own_ref[(2 * b + i) * own_v : (2 * b + i + 1) * own_v, :]
            u_out[b * own_v : (b + 1) * own_v, i, :] = u / beta_own


def flip(x, axes, mask):
    return lax.ppermute(x, axes, [(i, i ^ mask) for i in range(lax.axis_size(axes))])


def body(
    u_bases,
    v_bases,
    tile_ranks,
    u_unit,
    v_unit,
    x_solution,
    w_direction,
    alpha_prev,
    rhobar_prev,
    phibar_prev,
):
    tile_size = u_bases.shape[4]
    n_row = lax.axis_size("row")
    n_cplx = lax.axis_size("cplx")
    n_cols = lax.axis_size(("col", "cplx"))
    rows_total = tile_size * n_row
    cols_total = u_bases.shape[1] * tile_size * n_cols
    own_u, own_v = u_unit.shape[0], v_unit.shape[0]
    wide = v_unit.shape[2]
    rhs = own_v * n_row
    lanes = -(-rhs // 128) * 128
    block = 2 * own_v
    where = jnp.stack([lax.axis_index("row"), lax.axis_index(("col", "cplx"))]).astype(jnp.int32)

    (v_low,) = call(pack_kernel, [((block, wide), bf16)], v_unit)
    blocks = [v_low] + [flip(v_low, "row", k) for k in range(1, n_row)]
    low, own = call(
        partial(forward_kernel, n_row, own_v, own_u),
        [((2 * rhs, tile_size), bf16), ((2 * own_u, tile_size), f32)],
        where,
        tile_ranks,
        u_bases,
        v_bases,
        u_unit,
        alpha_prev[None],
        *blocks,
        scratch=[pltpu.VMEM((2 * rhs, tile_size), f32)],
    )
    got = [flip(low, "cplx", 1)]
    mask = n_cplx
    while mask < n_cols:
        low = (low.astype(f32) + got[-1].astype(f32)).astype(bf16)
        got.append(flip(low, ("col", "cplx"), mask + 1))
        mask *= 2
    *outs, own = call(
        partial(adjoint_kernel, n_row, len(got), own_v, own_u, lanes),
        [((block, wide + lanes), bf16)] * n_row + [((2 * own_u, tile_size), f32)],
        where,
        tile_ranks,
        u_bases,
        v_bases,
        own,
        low,
        *got,
        scratch=[pltpu.VMEM((8, 128), f32)],
    )
    blocks = [outs[0]] + [flip(outs[k], "row", k) for k in range(1, n_row)]
    devices = n_row * n_cols
    residual_v, beta, norms = call(
        partial(residual_kernel, n_row, rows_total, cols_total, lanes),
        [((block, wide), f32), ((1, lanes), f32), ((devices, lanes), f32)],
        where,
        v_unit,
        *blocks,
    )
    norms = lax.all_to_all(norms[:, None], ("row", "col", "cplx"), 0, 0)[:, 0]
    x_next, w_next, u_next, v_next, alpha, rhobar, phibar = call(
        partial(update_kernel, cols_total),
        [(x_solution.shape, f32), (w_direction.shape, f32), (u_unit.shape, f32), (v_unit.shape, f32)] + [((1, rhs), f32)] * 3,
        where,
        norms,
        beta,
        residual_v,
        own,
        x_solution,
        w_direction,
        rhobar_prev[None],
        phibar_prev[None],
    )
    return (x_next, w_next, u_next, v_next, alpha[0], rhobar[0], phibar[0])


def solution(mesh):
    placed = (
        P(("freq", "row"), ("col", "cplx"), None, None, None),
        P(("freq", "row"), ("col", "cplx"), None, None, None),
        P(("freq", "row"), ("col", "cplx")),
        P(("freq", "col", "cplx"), None, "row"),
        P(("freq", "row"), None, ("col", "cplx")),
        P(("freq", "row"), None, ("col", "cplx")),
        P(("freq", "row"), None, ("col", "cplx")),
        P("freq"),
        P("freq"),
        P("freq"),
    )
    return jax.shard_map(
        body,
        mesh=mesh,
        in_specs=placed,
        out_specs=(
            P(("freq", "row"), None, ("col", "cplx")),
            P(("freq", "row"), None, ("col", "cplx")),
            P(("freq", "col", "cplx"), None, "row"),
            P(("freq", "row"), None, ("col", "cplx")),
            P("freq"),
            P("freq"),
            P("freq"),
        ),
        check_vma=False,
    )
```

```python
from functools import partial

import jax
import jax.numpy as jnp
from jax import lax
from jax.experimental import pallas as pl
from jax.experimental.pallas import tpu as pltpu
from jax.sharding import PartitionSpec as P

epsilon = 1e-06
shrink = 2.0**-20
f32 = jnp.float32
bf16 = jnp.bfloat16


def call(kernel, outs, *args, scratch=(), vmem=12, hbm=False, cost=None):
    in_specs = [
        pl.BlockSpec(memory_space=pltpu.HBM if hbm else pltpu.SMEM if a.dtype == jnp.int32 else pltpu.VMEM) for a in args
    ]
    return pl.pallas_call(
        kernel,
        out_shape=[jax.ShapeDtypeStruct(s, d) for s, d in outs],
        in_specs=in_specs,
        out_specs=[pl.BlockSpec(memory_space=pltpu.VMEM)] * len(outs),
        scratch_shapes=list(scratch),
        compiler_params=pltpu.CompilerParams(vmem_limit_bytes=vmem * 2**20),
        cost_estimate=cost,
    )(*args)


def iota(shape, dim):
    return lax.broadcasted_iota(jnp.int32, shape, dim)


def to_lanes(column, place, lanes):
    rows = column.shape[0]
    here = iota((rows, lanes), 1) == place
    return jnp.sum(jnp.where(here, column, 0.0), axis=0, keepdims=True)


def to_column(lane_values, first, rows):
    lanes = lane_values.shape[1]
    here = iota((rows, lanes), 1) == iota((rows, lanes), 0) + first
    return jnp.sum(jnp.where(here, lane_values, 0.0), axis=1, keepdims=True)


def dot(a, b, transposed):
    return lax.dot_general(a, b, (((1,), (1 if transposed else 0,)), ((), ())), preferred_element_type=f32)


def through(inner, outer, ranks_ref, x, own):
    total = []
    tiles, _, ranks, size = inner.shape[1:]
    for q in range(tiles):
        g = dot(x(q), inner[0, q].reshape(2 * ranks, size), True)
        rows = g.shape[0]
        g = g.reshape(rows // (2 * own), 2, own, 2 * ranks)
        live = iota((1, 1, ranks), 2) < ranks_ref[0, q]
        re = jnp.where(live, g[:, 0, :, :ranks] + g[:, 1, :, ranks:], 0.0)
        im = jnp.where(live, g[:, 1, :, :ranks] - g[:, 0, :, ranks:], 0.0)
        both = jnp.stack([jnp.concatenate([re, -im], 2), jnp.concatenate([im, re], 2)], 1)
        both = both.reshape(rows, 2 * ranks).astype(bf16)
        total.append(dot(both, outer[0, q].reshape(2 * ranks, size), False))
    return total


def pack_kernel(v_ref, out_ref):
    own = v_ref.shape[0]
    out_ref[...] = jnp.concatenate([v_ref[:, 0, :], v_ref[:, 1, :]], 0).astype(bf16)


def load_kernel(many, *refs):
    ins, outs, sems = refs[:many], refs[many:-1], refs[-1]
    copies = [pltpu.make_async_copy(a, b, sems.at[i]) for i, (a, b) in enumerate(zip(ins, outs))]
    for copy in copies:
        copy.start()
    for copy in copies:
        copy.wait()


def forward_kernel(n_row, own_v, own_u, where_ref, ranks_ref, u_bases, v_bases, u_ref, alpha_ref, *refs):
    blocks, (low_ref, own_ref, total) = refs[:n_row], refs[n_row:]
    p, c = where_ref[0], where_ref[1]
    size = v_bases.shape[4]
    x = jnp.concatenate([b[...] for b in blocks], 0)
    parts = through(v_bases, u_bases, ranks_ref, lambda q: x[:, q * size : (q + 1) * size], own_v)
    total[...] = sum(parts[1:], parts[0])
    many = own_u // own_v
    for b in range(many):
        at = pl.ds(pl.multiple_of(((c * many + b) ^ p) * 2 * own_v, 2 * own_v), 2 * own_v)
        alpha = to_column(alpha_ref[0:1, :], c * own_u + b * own_v, own_v)
        mine = slice(b * own_v, (b + 1) * own_v)
        shift = jnp.concatenate([alpha * u_ref[mine, 0, :], alpha * u_ref[mine, 1, :]], 0)
        left = total[at, :] - shift
        own_ref[b * 2 * own_v : (b + 1) * 2 * own_v, :] = left
        total[at, :] = left
    low_ref[...] = total[...].astype(bf16)


def adjoint_kernel(n_row, n_got, own_v, own_u, lanes, where_ref, ranks_ref, u_bases, v_bases, own_ref, sum_ref, *refs):
    got, outs, own_out = refs[:n_got], refs[n_got : n_got + n_row], refs[n_got + n_row]
    p, c = where_ref[0], where_ref[1]
    many = own_u // own_v
    for b in range(many):
        at = pl.ds(pl.multiple_of(((c * many + b) ^ p) * 2 * own_v, 2 * own_v), 2 * own_v)
        mine = slice(b * 2 * own_v, (b + 1) * 2 * own_v)
        acc = own_ref[mine, :]
        for g in got:
            acc = acc + g[at, :].astype(f32)
        own_out[mine, :] = acc
    res = sum_ref[...].astype(f32) + got[-1][...].astype(f32)
    rows = res.shape[0]
    squares = jnp.sum(res * res, axis=1, keepdims=True)
    row = iota((rows, 1), 0)
    place = ((row // (2 * own_v)) ^ p) * own_v + row % own_v
    beta2 = to_lanes(squares, place, lanes)
    high = beta2.astype(bf16)
    low = (beta2 - high.astype(f32)).astype(bf16)
    tail = jnp.where(iota((2 * own_v, lanes), 0) == 0, high.astype(f32), low.astype(f32)).astype(bf16)
    x = (res * shrink).astype(bf16)
    parts = through(u_bases, v_bases, ranks_ref, lambda q: x, own_v)
    wide = parts[0].shape[1]
    for k, out in enumerate(outs):
        for q, part in enumerate(parts):
            out[:, q * wide : (q + 1) * wide] = part[k * 2 * own_v : (k + 1) * 2 * own_v].astype(bf16)
        out[:, len(parts) * wide :] = tail


def pairs(values):
    while len(values) > 1:
        values = [a + b for a, b in zip(values[::2], values[1::2])]
    return values[0]


def residual_kernel(n_row, rows_total, cols_total, lanes, where_ref, v_ref, *refs):
    blocks, (res_ref, beta_ref, norm_ref) = refs[:n_row], refs[n_row:]
    blocks = [blocks[0], blocks[-1], *blocks[1:-1]]
    p = where_ref[0]
    own_v, _, wide = v_ref.shape
    beta2 = pairs([b[0:1, wide:].astype(f32) + b[1:2, wide:].astype(f32) for b in blocks])
    beta = jnp.sqrt(beta2 / (2 * rows_total) + epsilon)
    beta_ref[...] = beta
    mine = to_column(beta, p * own_v, own_v)
    scale = rows_total / cols_total / shrink / mine
    squares = None
    for i in range(2):
        half = slice(i * own_v, (i + 1) * own_v)
        back = pairs([b[half, :wide].astype(f32) for b in blocks])
        res = scale * back - mine * v_ref[:, i, :]
        res_ref[half, :] = res
        here = jnp.sum(res * res, axis=1, keepdims=True)
        squares = here if squares is None else squares + here
    place = iota((own_v, 1), 0) + p * own_v
    norm_ref[...] = to_lanes(squares, place, lanes)


def turn(beta, scalars_ref):
    rhobar, phibar = scalars_ref[1:2, :], scalars_ref[2:3, :]
    rho = jnp.sqrt(rhobar * rhobar + beta * beta)
    return rho, rhobar / rho, beta / rho, phibar


def vectors_kernel(cols_total, where_ref, norms_ref, beta_ref, res_ref, own_ref, x_ref, w_ref, scalars_ref, x_out, w_out, u_out, v_out):
    p, c = where_ref[0], where_ref[1]
    own_v = x_ref.shape[0]
    own_u = u_out.shape[0]
    many = own_u // own_v
    rhs = scalars_ref.shape[1]
    beta = beta_ref[:, :rhs]
    rho, cosine, sine, phibar = turn(beta, scalars_ref)
    alpha2 = to_column(norms_ref[...], p * own_v, own_v)
    alpha = jnp.sqrt(alpha2 / (2 * cols_total) + epsilon)
    step_x = to_column(cosine * phibar / rho, p * own_v, own_v)
    step_w = to_column(sine / rho, p * own_v, own_v) * alpha
    for i in range(2):
        w = w_ref[:, i, :]
        v = res_ref[i * own_v : (i + 1) * own_v, :] / alpha
        x_out[:, i, :] = x_ref[:, i, :] + step_x * w
        v_out[:, i, :] = v
        w_out[:, i, :] = v - step_w * w
    for b in range(many):
        beta_own = to_column(beta, c * own_u + b * own_v, own_v)
        for i in range(2):
            u = own_ref[(2 * b + i) * own_v : (2 * b + i + 1) * own_v, :]
            u_out[b * own_v : (b + 1) * own_v, i, :] = u / beta_own


def scalars_kernel(n_row, cols_total, beta_ref, scalars_ref, *refs):
    norms, (alpha_out, rhobar_out, phibar_out) = refs[:n_row], refs[n_row:]
    rhs = scalars_ref.shape[1]
    rho, cosine, sine, phibar = turn(beta_ref[:, :rhs], scalars_ref)
    alpha2 = sum([n[...] for n in norms[1:]], norms[0][...])[:, :rhs]
    alpha = jnp.sqrt(alpha2 / (2 * cols_total) + epsilon)
    alpha_out[...] = alpha
    rhobar_out[...] = -cosine * alpha
    phibar_out[...] = sine * phibar


def flip(x, axes, mask):
    return lax.ppermute(x, axes, [(i, i ^ mask) for i in range(lax.axis_size(axes))])


def body(
    u_bases,
    v_bases,
    tile_ranks,
    u_unit,
    v_unit,
    x_solution,
    w_direction,
    alpha_prev,
    rhobar_prev,
    phibar_prev,
):
    tile_size = u_bases.shape[4]
    n_row = lax.axis_size("row")
    n_cplx = lax.axis_size("cplx")
    n_cols = lax.axis_size(("col", "cplx"))
    rows_total = tile_size * n_row
    cols_total = u_bases.shape[1] * tile_size * n_cols
    own_u, own_v = u_unit.shape[0], v_unit.shape[0]
    wide = v_unit.shape[2]
    rhs = own_v * n_row
    lanes = -(-rhs // 128) * 128
    block = 2 * own_v
    where = jnp.stack([lax.axis_index("row"), lax.axis_index(("col", "cplx"))]).astype(jnp.int32)

    vmem = 8 + rhs // 16
    scalars = jnp.stack([alpha_prev, rhobar_prev, phibar_prev])
    (v_low,) = call(pack_kernel, [((block, wide), bf16)], v_unit, cost=pl.CostEstimate(flops=10**10, bytes_accessed=2**26, transcendentals=0))
    blocks = [v_low] + [flip(v_low, "row", k) for k in range(1, n_row)]
    low, own = call(
        partial(forward_kernel, n_row, own_v, own_u),
        [((2 * rhs, tile_size), bf16), ((2 * own_u, tile_size), f32)],
        where,
        tile_ranks,
        u_bases,
        v_bases,
        u_unit,
        scalars,
        *blocks,
        scratch=[pltpu.VMEM((2 * rhs, tile_size), f32)],
        vmem=vmem,
    )
    got = [flip(low, "cplx", 1)]
    mask = n_cplx
    while mask < n_cols:
        low = (low.astype(f32) + got[-1].astype(f32)).astype(bf16)
        got.append(flip(low, ("col", "cplx"), mask + 1))
        mask *= 2
    *outs, own = call(
        partial(adjoint_kernel, n_row, len(got), own_v, own_u, lanes),
        [((block, wide + lanes), bf16)] * n_row + [((2 * own_u, tile_size), f32)],
        where,
        tile_ranks,
        u_bases,
        v_bases,
        own,
        low,
        *got,
        vmem=vmem,
    )
    order = [*range(2, n_row), 1]
    blocks = [outs[0]] + [flip(outs[k], "row", k) for k in order]
    residual_v, beta, norms = call(
        partial(residual_kernel, n_row, rows_total, cols_total, lanes),
        [((block, wide), f32), ((1, lanes), f32), ((1, lanes), f32)],
        where,
        v_unit,
        *blocks,
    )
    norms = norms + flip(norms, "cplx", 1)
    mask = n_cplx
    while mask < n_cols:
        norms = norms + flip(norms, ("col", "cplx"), mask + 1)
        mask *= 2
    norms_all = [norms] + [flip(norms, ("row", "col", "cplx"), k * n_cols + 1) for k in order]
    x_next, w_next, u_next, v_next = call(
        partial(vectors_kernel, cols_total),
        [(x_solution.shape, f32), (w_direction.shape, f32), (u_unit.shape, f32), (v_unit.shape, f32)],
        where,
        norms,
        beta,
        residual_v,
        own,
        x_solution,
        w_direction,
        scalars,
        cost=pl.CostEstimate(flops=10**9, bytes_accessed=2**23, transcendentals=0),
    )
    alpha, rhobar, phibar = call(
        partial(scalars_kernel, n_row, cols_total), [((1, rhs), f32)] * 3, beta, scalars, *norms_all
    )
    return (x_next, w_next, u_next, v_next, alpha[0], rhobar[0], phibar[0])


def solution(mesh):
    placed = (
        P(("freq", "row"), ("col", "cplx"), None, None, None),
        P(("freq", "row"), ("col", "cplx"), None, None, None),
        P(("freq", "row"), ("col", "cplx")),
        P(("freq", "col", "cplx"), None, "row"),
        P(("freq", "row"), None, ("col", "cplx")),
        P(("freq", "row"), None, ("col", "cplx")),
        P(("freq", "row"), None, ("col", "cplx")),
        P("freq"),
        P("freq"),
        P("freq"),
    )
    return jax.shard_map(
        body,
        mesh=mesh,
        in_specs=placed,
        out_specs=(
            P(("freq", "row"), None, ("col", "cplx")),
            P(("freq", "row"), None, ("col", "cplx")),
            P(("freq", "col", "cplx"), None, "row"),
            P(("freq", "row"), None, ("col", "cplx")),
            P("freq"),
            P("freq"),
            P("freq"),
        ),
        check_vma=False,
    )
```

```python
from functools import partial

import jax
import jax.numpy as jnp
from jax import lax
from jax.experimental import pallas as pl
from jax.experimental.pallas import tpu as pltpu
from jax.sharding import PartitionSpec as P

epsilon = 1e-06
shrink = 2.0**-20
f32 = jnp.float32
bf16 = jnp.bfloat16


def call(kernel, outs, *args, scratch=(), vmem=12, cost=None):
    in_specs = [pl.BlockSpec(memory_space=pltpu.VMEM)] * len(args)
    return pl.pallas_call(
        kernel,
        out_shape=[jax.ShapeDtypeStruct(s, d) for s, d in outs],
        in_specs=in_specs,
        out_specs=[pl.BlockSpec(memory_space=pltpu.VMEM)] * len(outs),
        scratch_shapes=list(scratch),
        compiler_params=pltpu.CompilerParams(vmem_limit_bytes=vmem * 2**20),
        cost_estimate=cost,
    )(*args)


def iota(shape, dim):
    return lax.broadcasted_iota(jnp.int32, shape, dim)


def to_lanes(column, place, lanes):
    rows = column.shape[0]
    here = iota((rows, lanes), 1) == place
    return jnp.sum(jnp.where(here, column, 0.0), axis=0, keepdims=True)


def to_column(lane_values, first, rows):
    lanes = lane_values.shape[1]
    here = iota((rows, lanes), 1) == iota((rows, lanes), 0) + first
    return jnp.sum(jnp.where(here, lane_values, 0.0), axis=1, keepdims=True)


def dot(a, b, transposed):
    return lax.dot_general(a, b, (((1,), (1 if transposed else 0,)), ((), ())), preferred_element_type=f32)


def through(inner, outer, live_ref, x, own):
    total = []
    tiles, _, ranks, size = inner.shape[1:]
    for q in range(tiles):
        g = dot(x(q), inner[0, q].reshape(2 * ranks, size), True)
        rows = g.shape[0]
        g = g.reshape(rows // (2 * own), 2, own, 2 * ranks)
        live = live_ref[q : q + 1, :]
        re = (g[:, 0, :, :ranks] + g[:, 1, :, ranks:]) * live
        im = (g[:, 1, :, :ranks] - g[:, 0, :, ranks:]) * live
        both = jnp.stack([jnp.concatenate([re, -im], 2), jnp.concatenate([im, re], 2)], 1)
        both = both.reshape(rows, 2 * ranks).astype(bf16)
        total.append(dot(both, outer[0, q].reshape(2 * ranks, size), False))
    return total


def in_order(blocks, order):
    return [blocks[0]] + [blocks[1 + order.index(k)] for k in range(1, len(blocks))]


def pack_kernel(v_ref, out_ref):
    own = v_ref.shape[0]
    out_ref[...] = jnp.concatenate([v_ref[:, 0, :], v_ref[:, 1, :]], 0).astype(bf16)


def forward_kernel(n_row, order, own_v, own_u, live_ref, u_bases, v_bases, u_ref, alpha_ref, *refs):
    blocks, (low_ref, own_ref, total) = in_order(refs[:n_row], order), refs[n_row:]
    p, c = lax.axis_index("row"), lax.axis_index(("col", "cplx"))
    size = v_bases.shape[4]
    x = jnp.concatenate([b[...] for b in blocks], 0)
    parts = through(v_bases, u_bases, live_ref, lambda q: x[:, q * size : (q + 1) * size], own_v)
    total[...] = sum(parts[1:], parts[0])
    many = own_u // own_v
    for b in range(many):
        at = pl.ds(pl.multiple_of(((c * many + b) ^ p) * 2 * own_v, 2 * own_v), 2 * own_v)
        alpha = to_column(alpha_ref[0:1, :], c * own_u + b * own_v, own_v)
        mine = slice(b * own_v, (b + 1) * own_v)
        shift = jnp.concatenate([alpha * u_ref[mine, 0, :], alpha * u_ref[mine, 1, :]], 0)
        left = total[at, :] - shift
        own_ref[b * 2 * own_v : (b + 1) * 2 * own_v, :] = left
        total[at, :] = left
    low_ref[...] = total[...].astype(bf16)


def adjoint_kernel(n_row, n_got, own_v, own_u, lanes, live_ref, u_bases, v_bases, own_ref, sum_ref, *refs):
    got, outs, own_out = refs[:n_got], refs[n_got : n_got + n_row], refs[n_got + n_row]
    p, c = lax.axis_index("row"), lax.axis_index(("col", "cplx"))
    many = own_u // own_v
    for b in range(many):
        at = pl.ds(pl.multiple_of(((c * many + b) ^ p) * 2 * own_v, 2 * own_v), 2 * own_v)
        mine = slice(b * 2 * own_v, (b + 1) * 2 * own_v)
        acc = own_ref[mine, :]
        for g in got:
            acc = acc + g[at, :].astype(f32)
        own_out[mine, :] = acc
    res = sum_ref[...].astype(f32) + got[-1][...].astype(f32)
    rows = res.shape[0]
    squares = jnp.sum(res * res, axis=1, keepdims=True)
    row = iota((rows, 1), 0)
    place = ((row // (2 * own_v)) ^ p) * own_v + row % own_v
    beta2 = to_lanes(squares, place, lanes)
    high = beta2.astype(bf16)
    low = (beta2 - high.astype(f32)).astype(bf16)
    tail = jnp.where(iota((2 * own_v, lanes), 0) == 0, high.astype(f32), low.astype(f32)).astype(bf16)
    x = (res * shrink).astype(bf16)
    parts = through(u_bases, v_bases, live_ref, lambda q: x, own_v)
    wide = parts[0].shape[1]
    for k, out in enumerate(outs):
        for q, part in enumerate(parts):
            out[:, q * wide : (q + 1) * wide] = part[k * 2 * own_v : (k + 1) * 2 * own_v].astype(bf16)
        out[:, len(parts) * wide :] = tail


def pairs(values):
    while len(values) > 1:
        values = [a + b for a, b in zip(values[::2], values[1::2])]
    return values[0]


def residual_kernel(n_row, order, rows_total, cols_total, lanes, v_ref, *refs):
    blocks, (res_ref, beta_ref, norm_ref) = in_order(refs[:n_row], order), refs[n_row:]
    p = lax.axis_index("row")
    own_v, _, wide = v_ref.shape
    beta2 = pairs([b[0:1, wide:].astype(f32) + b[1:2, wide:].astype(f32) for b in blocks])
    beta = jnp.sqrt(beta2 / (2 * rows_total) + epsilon)
    beta_ref[...] = beta
    mine = to_column(beta, p * own_v, own_v)
    scale = rows_total / cols_total / shrink / mine
    squares = None
    for i in range(2):
        half = slice(i * own_v, (i + 1) * own_v)
        back = pairs([b[half, :wide].astype(f32) for b in blocks])
        res = scale * back - mine * v_ref[:, i, :]
        res_ref[half, :] = res
        here = jnp.sum(res * res, axis=1, keepdims=True)
        squares = here if squares is None else squares + here
    place = iota((own_v, 1), 0) + p * own_v
    norm_ref[...] = to_lanes(squares, place, lanes)


def turn(beta, scalars_ref):
    rhobar, phibar = scalars_ref[1:2, :], scalars_ref[2:3, :]
    rho = jnp.sqrt(rhobar * rhobar + beta * beta)
    return rho, rhobar / rho, beta / rho, phibar


def vectors_kernel(cols_total, norms_ref, beta_ref, res_ref, own_ref, x_ref, w_ref, scalars_ref, x_out, w_out, u_out, v_out):
    p, c = lax.axis_index("row"), lax.axis_index(("col", "cplx"))
    own_v = x_ref.shape[0]
    own_u = u_out.shape[0]
    many = own_u // own_v
    rhs = scalars_ref.shape[1]
    beta = beta_ref[:, :rhs]
    rho, cosine, sine, phibar = turn(beta, scalars_ref)
    alpha2 = to_column(norms_ref[...], p * own_v, own_v)
    alpha = jnp.sqrt(alpha2 / (2 * cols_total) + epsilon)
    step_x = to_column(cosine * phibar / rho, p * own_v, own_v)
    step_w = to_column(sine / rho, p * own_v, own_v) * alpha
    for i in range(2):
        w = w_ref[:, i, :]
        v = res_ref[i * own_v : (i + 1) * own_v, :] / alpha
        x_out[:, i, :] = x_ref[:, i, :] + step_x * w
        v_out[:, i, :] = v
        w_out[:, i, :] = v - step_w * w
    for b in range(many):
        beta_own = to_column(beta, c * own_u + b * own_v, own_v)
        for i in range(2):
            u = own_ref[(2 * b + i) * own_v : (2 * b + i + 1) * own_v, :]
            u_out[b * own_v : (b + 1) * own_v, i, :] = u / beta_own


def scalars_kernel(n_row, cols_total, beta_ref, scalars_ref, *refs):
    norms, (alpha_out, rhobar_out, phibar_out) = refs[:n_row], refs[n_row:]
    rhs = scalars_ref.shape[1]
    rho, cosine, sine, phibar = turn(beta_ref[:, :rhs], scalars_ref)
    alpha2 = sum([n[...] for n in norms[1:]], norms[0][...])[:, :rhs]
    alpha = jnp.sqrt(alpha2 / (2 * cols_total) + epsilon)
    alpha_out[...] = alpha
    rhobar_out[...] = -cosine * alpha
    phibar_out[...] = sine * phibar


def flip(x, axes, mask):
    return lax.ppermute(x, axes, [(i, i ^ mask) for i in range(lax.axis_size(axes))])


def body(
    u_bases,
    v_bases,
    tile_ranks,
    u_unit,
    v_unit,
    x_solution,
    w_direction,
    alpha_prev,
    rhobar_prev,
    phibar_prev,
):
    tile_size = u_bases.shape[4]
    n_row = lax.axis_size("row")
    n_cplx = lax.axis_size("cplx")
    n_cols = lax.axis_size(("col", "cplx"))
    rows_total = tile_size * n_row
    cols_total = u_bases.shape[1] * tile_size * n_cols
    own_u, own_v = u_unit.shape[0], v_unit.shape[0]
    wide = v_unit.shape[2]
    rhs = own_v * n_row
    lanes = -(-rhs // 128) * 128
    block = 2 * own_v
    live = (jnp.arange(u_bases.shape[3], dtype=jnp.int32)[None] < tile_ranks[0][:, None]).astype(f32)

    vmem = 8 + rhs // 16
    first = [1, *range(n_row - 1, 1, -1)]
    second = [*range(2, n_row), 1]
    third = first
    scalars = jnp.stack([alpha_prev, rhobar_prev, phibar_prev])
    (v_low,) = call(pack_kernel, [((block, wide), bf16)], v_unit, cost=pl.CostEstimate(flops=10**10, bytes_accessed=2**26, transcendentals=0))
    blocks = [v_low] + [flip(v_low, "row", k) for k in first]
    low, own = call(
        partial(forward_kernel, n_row, first, own_v, own_u),
        [((2 * rhs, tile_size), bf16), ((2 * own_u, tile_size), f32)],
        live,
        u_bases,
        v_bases,
        u_unit,
        scalars,
        *blocks,
        scratch=[pltpu.VMEM((2 * rhs, tile_size), f32)],
        vmem=vmem,
    )
    got = [flip(low, "cplx", 1)]
    mask = n_cplx
    while mask < n_cols:
        low = (low.astype(f32) + got[-1].astype(f32)).astype(bf16)
        got.append(flip(low, ("col", "cplx"), mask + 1))
        mask *= 2
    *outs, own = call(
        partial(adjoint_kernel, n_row, len(got), own_v, own_u, lanes),
        [((block, wide + lanes), bf16)] * n_row + [((2 * own_u, tile_size), f32)],
        live,
        u_bases,
        v_bases,
        own,
        low,
        *got,
        vmem=vmem,
    )
    blocks = [outs[0]] + [flip(outs[k], "row", k) for k in second]
    residual_v, beta, norms = call(
        partial(residual_kernel, n_row, second, rows_total, cols_total, lanes),
        [((block, wide), f32), ((1, lanes), f32), ((1, lanes), f32)],
        v_unit,
        *blocks,
    )
    norms = norms + flip(norms, "cplx", 1)
    mask = n_cplx
    while mask < n_cols:
        norms = norms + flip(norms, ("col", "cplx"), mask + 1)
        mask *= 2
    norms_all = [norms] + [flip(norms, ("row", "col", "cplx"), k * n_cols + 1) for k in third]
    x_next, w_next, u_next, v_next = call(
        partial(vectors_kernel, cols_total),
        [(x_solution.shape, f32), (w_direction.shape, f32), (u_unit.shape, f32), (v_unit.shape, f32)],
        norms,
        beta,
        residual_v,
        own,
        x_solution,
        w_direction,
        scalars,
        cost=pl.CostEstimate(flops=10**9, bytes_accessed=2**23, transcendentals=0),
    )
    alpha, rhobar, phibar = call(
        partial(scalars_kernel, n_row, cols_total), [((1, rhs), f32)] * 3, beta, scalars, *norms_all
    )
    return (x_next, w_next, u_next, v_next, alpha[0], rhobar[0], phibar[0])


def solution(mesh):
    placed = (
        P(("freq", "row"), ("col", "cplx"), None, None, None),
        P(("freq", "row"), ("col", "cplx"), None, None, None),
        P(("freq", "row"), ("col", "cplx")),
        P(("freq", "col", "cplx"), None, "row"),
        P(("freq", "row"), None, ("col", "cplx")),
        P(("freq", "row"), None, ("col", "cplx")),
        P(("freq", "row"), None, ("col", "cplx")),
        P("freq"),
        P("freq"),
        P("freq"),
    )
    return jax.shard_map(
        body,
        mesh=mesh,
        in_specs=placed,
        out_specs=(
            P(("freq", "row"), None, ("col", "cplx")),
            P(("freq", "row"), None, ("col", "cplx")),
            P(("freq", "col", "cplx"), None, "row"),
            P(("freq", "row"), None, ("col", "cplx")),
            P("freq"),
            P("freq"),
            P("freq"),
        ),
        check_vma=False,
    )
```

```python
from functools import partial

import jax
import jax.numpy as jnp
from jax import lax
from jax.experimental import pallas as pl
from jax.experimental.pallas import tpu as pltpu
from jax.sharding import PartitionSpec as P

epsilon = 1e-06
shrink = 2.0**-20
f32 = jnp.float32
bf16 = jnp.bfloat16


def call(kernel, outs, *args, scratch=(), vmem=12, cost=None):
    in_specs = [pl.BlockSpec(memory_space=pltpu.VMEM)] * len(args)
    return pl.pallas_call(
        kernel,
        out_shape=[jax.ShapeDtypeStruct(s, d) for s, d in outs],
        in_specs=in_specs,
        out_specs=[pl.BlockSpec(memory_space=pltpu.VMEM)] * len(outs),
        scratch_shapes=list(scratch),
        compiler_params=pltpu.CompilerParams(vmem_limit_bytes=vmem * 2**20),
        cost_estimate=cost,
    )(*args)


def iota(shape, dim):
    return lax.broadcasted_iota(jnp.int32, shape, dim)


def to_lanes(column, place, lanes):
    rows = column.shape[0]
    here = iota((rows, lanes), 1) == place
    return jnp.sum(jnp.where(here, column, 0.0), axis=0, keepdims=True)


def to_column(lane_values, first, rows):
    lanes = lane_values.shape[1]
    here = iota((rows, lanes), 1) == iota((rows, lanes), 0) + first
    return jnp.sum(jnp.where(here, lane_values, 0.0), axis=1, keepdims=True)


def dot(a, b, transposed):
    return lax.dot_general(a, b, (((1,), (1 if transposed else 0,)), ((), ())), preferred_element_type=f32)


def through(inner, outer, live_ref, x, own):
    total = []
    tiles, _, ranks, size = inner.shape[1:]
    for q in range(tiles):
        g = dot(x(q), inner[0, q].reshape(2 * ranks, size), True)
        rows = g.shape[0]
        g = g.reshape(rows // (2 * own), 2, own, 2 * ranks)
        live = live_ref[q : q + 1, :]
        re = (g[:, 0, :, :ranks] + g[:, 1, :, ranks:]) * live
        im = (g[:, 1, :, :ranks] - g[:, 0, :, ranks:]) * live
        both = jnp.stack([jnp.concatenate([re, -im], 2), jnp.concatenate([im, re], 2)], 1)
        both = both.reshape(rows, 2 * ranks).astype(bf16)
        total.append(dot(both, outer[0, q].reshape(2 * ranks, size), False))
    return total


def in_order(blocks, order):
    return [blocks[0]] + [blocks[1 + order.index(k)] for k in range(1, len(blocks))]


def pack_kernel(v_ref, out_ref):
    own = v_ref.shape[0]
    out_ref[...] = jnp.concatenate([v_ref[:, 0, :], v_ref[:, 1, :]], 0).astype(bf16)


def forward_kernel(n_row, order, own_v, own_u, live_ref, u_bases, v_bases, u_ref, alpha_ref, *refs):
    blocks, (low_ref, own_ref, kept_ref, total) = in_order(refs[:n_row], order), refs[n_row:]
    p, c = lax.axis_index("row"), lax.axis_index(("col", "cplx"))
    size = v_bases.shape[4]
    x = jnp.concatenate([b[...] for b in blocks], 0)
    kept_ref[0] = blocks[0][...]
    kept_ref[1] = blocks[n_row // 2][...]
    parts = through(v_bases, u_bases, live_ref, lambda q: x[:, q * size : (q + 1) * size], own_v)
    total[...] = sum(parts[1:], parts[0])
    many = own_u // own_v
    for b in range(many):
        at = pl.ds(pl.multiple_of(((c * many + b) ^ p) * 2 * own_v, 2 * own_v), 2 * own_v)
        alpha = to_column(alpha_ref[0:1, :], c * own_u + b * own_v, own_v)
        mine = slice(b * own_v, (b + 1) * own_v)
        shift = jnp.concatenate([alpha * u_ref[mine, 0, :], alpha * u_ref[mine, 1, :]], 0)
        left = total[at, :] - shift
        own_ref[b * 2 * own_v : (b + 1) * 2 * own_v, :] = left
        total[at, :] = left
    low_ref[...] = total[...].astype(bf16)


def adjoint_kernel(n_row, n_got, own_v, own_u, lanes, live_ref, u_bases, v_bases, own_ref, sum_ref, *refs):
    got, outs, own_out = refs[:n_got], refs[n_got : n_got + n_row], refs[n_got + n_row]
    p, c = lax.axis_index("row"), lax.axis_index(("col", "cplx"))
    many = own_u // own_v
    for b in range(many):
        at = pl.ds(pl.multiple_of(((c * many + b) ^ p) * 2 * own_v, 2 * own_v), 2 * own_v)
        mine = slice(b * 2 * own_v, (b + 1) * 2 * own_v)
        acc = own_ref[mine, :]
        for g in got:
            acc = acc + g[at, :].astype(f32)
        own_out[mine, :] = acc
    res = sum_ref[...].astype(f32) + got[-1][...].astype(f32)
    rows = res.shape[0]
    squares = jnp.sum(res * res, axis=1, keepdims=True)
    row = iota((rows, 1), 0)
    place = ((row // (2 * own_v)) ^ p) * own_v + row % own_v
    beta2 = to_lanes(squares, place, lanes)
    high = beta2.astype(bf16)
    low = (beta2 - high.astype(f32)).astype(bf16)
    tail = jnp.where(iota((16, lanes), 0) == 0, high.astype(f32), low.astype(f32)).astype(bf16)
    x = (res * shrink).astype(bf16)
    parts = through(u_bases, v_bases, live_ref, lambda q: x, own_v)
    wide = jnp.concatenate(parts, 1).astype(bf16)
    strips = wide.shape[1] // lanes
    for k, out in enumerate(outs):
        for i, j in enumerate((k, k ^ (n_row // 2))):
            for t in range(strips):
                at = (i * strips + t) * 2 * own_v
                out[at : at + 2 * own_v, :] = wide[j * 2 * own_v : (j + 1) * 2 * own_v, t * lanes : (t + 1) * lanes]
        out[2 * strips * 2 * own_v :, :] = tail


def pairs(values):
    while len(values) > 1:
        values = [a + b for a, b in zip(values[::2], values[1::2])]
    return values[0]


def residual_kernel(n_row, order, rows_total, cols_total, lanes, v_ref, kept_ref, *refs):
    blocks, (res_ref, beta_ref, norm_ref) = in_order(refs[:n_row], order), refs[n_row:]
    p = lax.axis_index("row")
    own_v, _, wide = v_ref.shape
    strips = wide // lanes
    end = 2 * strips * 2 * own_v
    beta2 = pairs([b[end : end + 1, :].astype(f32) + b[end + 1 : end + 2, :].astype(f32) for b in blocks])
    beta = jnp.sqrt(beta2 / (2 * rows_total) + epsilon)
    beta_ref[...] = beta
    norms = jnp.zeros((1, lanes), f32)
    for h, row in enumerate((p, p ^ (n_row // 2))):
        beta_here = to_column(beta, row * own_v, own_v)
        beta_here = jnp.concatenate([beta_here, beta_here], 0)
        scale = rows_total / cols_total / shrink / beta_here
        squares = jnp.zeros((own_v, lanes), f32)
        for t in range(strips):
            at = (h * strips + t) * 2 * own_v
            back = scale * pairs([b[at : at + 2 * own_v, :].astype(f32) for b in blocks])
            strip = slice(t * lanes, (t + 1) * lanes)
            low = beta_here * kept_ref[h, :, strip].astype(f32)
            for i in range(2):
                half = slice(i * own_v, (i + 1) * own_v)
                if h == 0:
                    res_ref[half, strip] = back[half] - beta_here[half] * v_ref[:, i, strip]
                res = back[half] - low[half]
                squares = squares + res * res
        squares = jnp.sum(squares, axis=1, keepdims=True)
        place = iota((own_v, 1), 0) + row * own_v
        norms = norms + to_lanes(squares, place, lanes)
    norm_ref[...] = norms


def turn(beta, scalars_ref):
    rhobar, phibar = scalars_ref[1:2, :], scalars_ref[2:3, :]
    rho = jnp.sqrt(rhobar * rhobar + beta * beta)
    return rho, rhobar / rho, beta / rho, phibar


def vectors_kernel(cols_total, norms_ref, got_ref, beta_ref, res_ref, own_ref, x_ref, w_ref, scalars_ref, x_out, w_out, u_out, v_out, sum_out):
    p, c = lax.axis_index("row"), lax.axis_index(("col", "cplx"))
    own_v = x_ref.shape[0]
    own_u = u_out.shape[0]
    many = own_u // own_v
    rhs = scalars_ref.shape[1]
    beta = beta_ref[:, :rhs]
    rho, cosine, sine, phibar = turn(beta, scalars_ref)
    norms = norms_ref[...] + got_ref[...]
    sum_out[...] = norms
    alpha2 = to_column(norms, p * own_v, own_v)
    alpha = jnp.sqrt(alpha2 / (2 * cols_total) + epsilon)
    step_x = to_column(cosine * phibar / rho, p * own_v, own_v)
    step_w = to_column(sine / rho, p * own_v, own_v) * alpha
    for i in range(2):
        w = w_ref[:, i, :]
        v = res_ref[i * own_v : (i + 1) * own_v, :] / alpha
        x_out[:, i, :] = x_ref[:, i, :] + step_x * w
        v_out[:, i, :] = v
        w_out[:, i, :] = v - step_w * w
    for b in range(many):
        beta_own = to_column(beta, c * own_u + b * own_v, own_v)
        for i in range(2):
            u = own_ref[(2 * b + i) * own_v : (2 * b + i + 1) * own_v, :]
            u_out[b * own_v : (b + 1) * own_v, i, :] = u / beta_own


def scalars_kernel(cols_total, beta_ref, scalars_ref, *refs):
    norms, (alpha_out, rhobar_out, phibar_out) = refs[:-3], refs[-3:]
    rhs = scalars_ref.shape[1]
    rho, cosine, sine, phibar = turn(beta_ref[:, :rhs], scalars_ref)
    alpha2 = sum([n[...] for n in norms[1:]], norms[0][...])[:, :rhs]
    alpha = jnp.sqrt(alpha2 / (2 * cols_total) + epsilon)
    alpha_out[...] = alpha
    rhobar_out[...] = -cosine * alpha
    phibar_out[...] = sine * phibar


def third_of(x):
    return x


def flip(x, axes, mask):
    return lax.ppermute(x, axes, [(i, i ^ mask) for i in range(lax.axis_size(axes))])


def body(
    u_bases,
    v_bases,
    tile_ranks,
    u_unit,
    v_unit,
    x_solution,
    w_direction,
    alpha_prev,
    rhobar_prev,
    phibar_prev,
):
    tile_size = u_bases.shape[4]
    n_row = lax.axis_size("row")
    n_cplx = lax.axis_size("cplx")
    n_cols = lax.axis_size(("col", "cplx"))
    rows_total = tile_size * n_row
    cols_total = u_bases.shape[1] * tile_size * n_cols
    own_u, own_v = u_unit.shape[0], v_unit.shape[0]
    wide = v_unit.shape[2]
    rhs = own_v * n_row
    lanes = -(-rhs // 128) * 128
    block = 2 * own_v
    live = (jnp.arange(u_bases.shape[3], dtype=jnp.int32)[None] < tile_ranks[0][:, None]).astype(f32)

    vmem = 8 + rhs // 16
    first = [1, *range(n_row - 1, 1, -1)]
    second = [2, 1, *range(3, n_row)]
    scalars = jnp.stack([alpha_prev, rhobar_prev, phibar_prev])
    (v_low,) = call(pack_kernel, [((block, wide), bf16)], v_unit, cost=pl.CostEstimate(flops=10**10, bytes_accessed=2**26, transcendentals=0))
    blocks = [v_low] + [flip(v_low, "row", k) for k in first]
    low, own, kept = call(
        partial(forward_kernel, n_row, first, own_v, own_u),
        [((2 * rhs, tile_size), bf16), ((2 * own_u, tile_size), f32), ((2, block, wide), bf16)],
        live,
        u_bases,
        v_bases,
        u_unit,
        scalars,
        *blocks,
        scratch=[pltpu.VMEM((2 * rhs, tile_size), f32)],
        vmem=vmem,
    )
    got = [flip(low, "cplx", 1)]
    mask = n_cplx
    while mask < n_cols:
        low = (low.astype(f32) + got[-1].astype(f32)).astype(bf16)
        got.append(flip(low, ("col", "cplx"), mask + 1))
        mask *= 2
    *outs, own = call(
        partial(adjoint_kernel, n_row, len(got), own_v, own_u, lanes),
        [((2 * block * (wide // lanes) + 16, lanes), bf16)] * n_row + [((2 * own_u, tile_size), f32)],
        live,
        u_bases,
        v_bases,
        own,
        low,
        *got,
        vmem=vmem,
    )
    sums = [outs[0]] + [flip(outs[k], "row", k) for k in second]
    residual_v, beta, norms = call(
        partial(residual_kernel, n_row, second, rows_total, cols_total, lanes),
        [((block, wide), f32), ((1, lanes), f32), ((1, lanes), f32)],
        v_unit,
        kept,
        *sums,
    )
    norms = norms + flip(norms, "cplx", 1)
    mask = n_cplx
    while 2 * mask < n_cols:
        norms = norms + flip(norms, ("col", "cplx"), mask + 1)
        mask *= 2
    across = [mask] + [k * n_cols + m for k in range(1, n_row // 2) for m in (0, mask)]
    got = [flip(norms, ("row", "col", "cplx"), m + 1) for m in across]
    x_next, w_next, u_next, v_next, norms = call(
        partial(vectors_kernel, cols_total),
        [(x_solution.shape, f32), (w_direction.shape, f32), (u_unit.shape, f32), (v_unit.shape, f32), ((1, lanes), f32)],
        norms,
        got[0],
        beta,
        residual_v,
        own,
        x_solution,
        w_direction,
        scalars,
        cost=pl.CostEstimate(flops=10**9, bytes_accessed=2**23, transcendentals=0),
    )
    alpha, rhobar, phibar = call(
        partial(scalars_kernel, cols_total), [((1, rhs), f32)] * 3, beta, scalars, norms, *third_of(got[1:])
    )
    return (x_next, w_next, u_next, v_next, alpha[0], rhobar[0], phibar[0])


def solution(mesh):
    placed = (
        P(("freq", "row"), ("col", "cplx"), None, None, None),
        P(("freq", "row"), ("col", "cplx"), None, None, None),
        P(("freq", "row"), ("col", "cplx")),
        P(("freq", "col", "cplx"), None, "row"),
        P(("freq", "row"), None, ("col", "cplx")),
        P(("freq", "row"), None, ("col", "cplx")),
        P(("freq", "row"), None, ("col", "cplx")),
        P("freq"),
        P("freq"),
        P("freq"),
    )
    return jax.shard_map(
        body,
        mesh=mesh,
        in_specs=placed,
        out_specs=(
            P(("freq", "row"), None, ("col", "cplx")),
            P(("freq", "row"), None, ("col", "cplx")),
            P(("freq", "col", "cplx"), None, "row"),
            P(("freq", "row"), None, ("col", "cplx")),
            P("freq"),
            P("freq"),
            P("freq"),
        ),
        check_vma=False,
    )
```

```python
from functools import partial

import jax
import jax.numpy as jnp
from jax import lax
from jax.experimental import pallas as pl
from jax.experimental.pallas import tpu as pltpu
from jax.sharding import PartitionSpec as P

epsilon = 1e-06
shrink = 2.0**-20
f32 = jnp.float32
bf16 = jnp.bfloat16


def call(kernel, outs, *args, scratch=(), vmem=12, cost=None):
    in_specs = [pl.BlockSpec(memory_space=pltpu.VMEM)] * len(args)
    return pl.pallas_call(
        kernel,
        out_shape=[jax.ShapeDtypeStruct(s, d) for s, d in outs],
        in_specs=in_specs,
        out_specs=[pl.BlockSpec(memory_space=pltpu.VMEM)] * len(outs),
        scratch_shapes=list(scratch),
        compiler_params=pltpu.CompilerParams(vmem_limit_bytes=vmem * 2**20),
        cost_estimate=cost,
    )(*args)


def iota(shape, dim):
    return lax.broadcasted_iota(jnp.int32, shape, dim)


def to_lanes(column, place, lanes):
    rows = column.shape[0]
    here = iota((rows, lanes), 1) == place
    return jnp.sum(jnp.where(here, column, 0.0), axis=0, keepdims=True)


def to_column(lane_values, first, rows):
    lanes = lane_values.shape[1]
    here = iota((rows, lanes), 1) == iota((rows, lanes), 0) + first
    return jnp.sum(jnp.where(here, lane_values, 0.0), axis=1, keepdims=True)


def dot(a, b, transposed):
    return lax.dot_general(a, b, (((1,), (1 if transposed else 0,)), ((), ())), preferred_element_type=f32)


def through(inner, outer, live_ref, x, own):
    tiles, _, ranks, size = inner.shape[1:]
    mids = []
    gs = [dot(x(q), inner[0, q].reshape(2 * ranks, size), True) for q in range(tiles)]
    for q, g in enumerate(gs):
        rows = g.shape[0]
        g = g.reshape(rows // (2 * own), 2, own, 2 * ranks)
        live = live_ref[q : q + 1, :]
        re = (g[:, 0, :, :ranks] + g[:, 1, :, ranks:]) * live
        im = (g[:, 1, :, :ranks] - g[:, 0, :, ranks:]) * live
        both = jnp.stack([jnp.concatenate([re, -im], 2), jnp.concatenate([im, re], 2)], 1)
        mids.append(both.reshape(rows, 2 * ranks).astype(bf16))
    return [dot(both, outer[0, q].reshape(2 * ranks, size), False) for q, both in enumerate(mids)]


def in_order(blocks, order):
    return [blocks[0]] + [blocks[1 + order.index(k)] for k in range(1, len(blocks))]


def prepare_kernel(ranks_ref, alpha_ref, rhobar_ref, phibar_ref, live_ref, scalars_ref):
    for q in range(live_ref.shape[0]):
        here = iota((1, live_ref.shape[1]), 1) < ranks_ref[0:1, q : q + 1]
        live_ref[q : q + 1, :] = here.astype(f32)
    for i, ref in enumerate((alpha_ref, rhobar_ref, phibar_ref)):
        scalars_ref[i : i + 1, :] = ref[...]


def forward_kernel(n_row, order, own_v, own_u, live_ref, u_bases, v_bases, u_ref, alpha_ref, *refs):
    blocks, (low_ref, own_ref, kept_ref, total) = in_order(refs[:n_row], order), refs[n_row:]
    p, c = lax.axis_index("row"), lax.axis_index(("col", "cplx"))
    size = v_bases.shape[4]
    x = jnp.concatenate([b[...] for b in blocks], 0)
    kept_ref[0] = blocks[0][...]
    kept_ref[1] = blocks[n_row // 2][...]
    parts = through(v_bases, u_bases, live_ref, lambda q: x[:, q * size : (q + 1) * size], own_v)
    total[...] = sum(parts[1:], parts[0])
    many = own_u // own_v
    for b in range(many):
        at = pl.ds(pl.multiple_of(((c * many + b) ^ p) * 2 * own_v, 2 * own_v), 2 * own_v)
        alpha = to_column(alpha_ref[0:1, :], c * own_u + b * own_v, own_v)
        mine = slice(b * own_v, (b + 1) * own_v)
        shift = jnp.concatenate([alpha * u_ref[mine, 0, :], alpha * u_ref[mine, 1, :]], 0)
        left = total[at, :] - shift
        own_ref[b * 2 * own_v : (b + 1) * 2 * own_v, :] = left
        total[at, :] = left
    low_ref[...] = total[...].astype(bf16)


def adjoint_kernel(n_row, n_got, own_v, own_u, lanes, live_ref, u_bases, v_bases, own_ref, sum_ref, *refs):
    got, outs, own_out = refs[:n_got], refs[n_got : n_got + n_row], refs[n_got + n_row]
    p, c = lax.axis_index("row"), lax.axis_index(("col", "cplx"))
    many = own_u // own_v
    for b in range(many):
        at = pl.ds(pl.multiple_of(((c * many + b) ^ p) * 2 * own_v, 2 * own_v), 2 * own_v)
        mine = slice(b * 2 * own_v, (b + 1) * 2 * own_v)
        acc = own_ref[mine, :]
        for g in got:
            acc = acc + g[at, :].astype(f32)
        own_out[mine, :] = acc
    res = sum_ref[...].astype(f32) + got[-1][...].astype(f32)
    rows = res.shape[0]
    squares = jnp.sum(res * res, axis=1, keepdims=True)
    row = iota((rows, 1), 0)
    place = ((row // (2 * own_v)) ^ p) * own_v + row % own_v
    beta2 = to_lanes(squares, place, lanes)
    high = beta2.astype(bf16)
    low = (beta2 - high.astype(f32)).astype(bf16)
    tail = jnp.where(iota((16, lanes), 0) == 0, high.astype(f32), low.astype(f32)).astype(bf16)
    x = (res * shrink).astype(bf16)
    parts = through(u_bases, v_bases, live_ref, lambda q: x, own_v)
    wide = jnp.concatenate(parts, 1).astype(bf16)
    strips = wide.shape[1] // lanes
    for k, out in enumerate(outs):
        for i, j in enumerate((k, k ^ (n_row // 2))):
            for t in range(strips):
                at = (i * strips + t) * 2 * own_v
                out[at : at + 2 * own_v, :] = wide[j * 2 * own_v : (j + 1) * 2 * own_v, t * lanes : (t + 1) * lanes]
        out[2 * strips * 2 * own_v :, :] = tail


def pairs(values):
    while len(values) > 1:
        values = [a + b for a, b in zip(values[::2], values[1::2])]
    return values[0]


def residual_kernel(n_row, order, rows_total, cols_total, lanes, v_ref, kept_ref, *refs):
    blocks, (res_ref, beta_ref, norm_ref) = in_order(refs[:n_row], order), refs[n_row:]
    p = lax.axis_index("row")
    own_v, _, wide = v_ref.shape
    strips = wide // lanes
    end = 2 * strips * 2 * own_v
    beta2 = pairs([b[end : end + 1, :].astype(f32) + b[end + 1 : end + 2, :].astype(f32) for b in blocks])
    beta = jnp.sqrt(beta2 / (2 * rows_total) + epsilon)
    beta_ref[...] = beta
    norms = jnp.zeros((1, lanes), f32)
    for h, row in enumerate((p, p ^ (n_row // 2))):
        beta_here = to_column(beta, row * own_v, own_v)
        beta_here = jnp.concatenate([beta_here, beta_here], 0)
        scale = rows_total / cols_total / shrink / beta_here
        squares = jnp.zeros((own_v, lanes), f32)
        for t in range(strips):
            at = (h * strips + t) * 2 * own_v
            back = scale * pairs([b[at : at + 2 * own_v, :].astype(f32) for b in blocks])
            strip = slice(t * lanes, (t + 1) * lanes)
            low = beta_here * kept_ref[h, :, strip].astype(f32)
            for i in range(2):
                half = slice(i * own_v, (i + 1) * own_v)
                if h == 0:
                    res_ref[half, strip] = back[half] - beta_here[half] * v_ref[:, i, strip]
                res = back[half] - low[half]
                squares = squares + res * res
        squares = jnp.sum(squares, axis=1, keepdims=True)
        place = iota((own_v, 1), 0) + row * own_v
        norms = norms + to_lanes(squares, place, lanes)
    norm_ref[...] = norms


def turn(beta, scalars_ref):
    rhobar, phibar = scalars_ref[1:2, :], scalars_ref[2:3, :]
    rho = jnp.sqrt(rhobar * rhobar + beta * beta)
    return rho, rhobar / rho, beta / rho, phibar


def vectors_kernel(cols_total, norms_ref, got_ref, beta_ref, res_ref, own_ref, x_ref, w_ref, scalars_ref, x_out, w_out, u_out, v_out, sum_out):
    p, c = lax.axis_index("row"), lax.axis_index(("col", "cplx"))
    own_v = x_ref.shape[0]
    own_u = u_out.shape[0]
    many = own_u // own_v
    rhs = scalars_ref.shape[1]
    beta = beta_ref[:, :rhs]
    rho, cosine, sine, phibar = turn(beta, scalars_ref)
    norms = norms_ref[...] + got_ref[...]
    sum_out[...] = norms
    alpha2 = to_column(norms, p * own_v, own_v)
    alpha = jnp.sqrt(alpha2 / (2 * cols_total) + epsilon)
    step_x = to_column(cosine * phibar / rho, p * own_v, own_v)
    step_w = to_column(sine / rho, p * own_v, own_v) * alpha
    for i in range(2):
        w = w_ref[:, i, :]
        v = res_ref[i * own_v : (i + 1) * own_v, :] / alpha
        x_out[:, i, :] = x_ref[:, i, :] + step_x * w
        v_out[:, i, :] = v
        w_out[:, i, :] = v - step_w * w
    for b in range(many):
        beta_own = to_column(beta, c * own_u + b * own_v, own_v)
        for i in range(2):
            u = own_ref[(2 * b + i) * own_v : (2 * b + i + 1) * own_v, :]
            u_out[b * own_v : (b + 1) * own_v, i, :] = u / beta_own


def scalars_kernel(cols_total, beta_ref, scalars_ref, *refs):
    norms, (alpha_out, rhobar_out, phibar_out) = refs[:-3], refs[-3:]
    rhs = scalars_ref.shape[1]
    rho, cosine, sine, phibar = turn(beta_ref[:, :rhs], scalars_ref)
    alpha2 = sum([n[...] for n in norms[1:]], norms[0][...])[:, :rhs]
    alpha = jnp.sqrt(alpha2 / (2 * cols_total) + epsilon)
    alpha_out[...] = alpha
    rhobar_out[...] = -cosine * alpha
    phibar_out[...] = sine * phibar


def third_of(x):
    return x


def flip(x, axes, mask):
    return lax.ppermute(x, axes, [(i, i ^ mask) for i in range(lax.axis_size(axes))])


def body(
    u_bases,
    v_bases,
    tile_ranks,
    u_unit,
    v_unit,
    x_solution,
    w_direction,
    alpha_prev,
    rhobar_prev,
    phibar_prev,
):
    tile_size = u_bases.shape[4]
    n_row = lax.axis_size("row")
    n_cplx = lax.axis_size("cplx")
    n_cols = lax.axis_size(("col", "cplx"))
    rows_total = tile_size * n_row
    cols_total = u_bases.shape[1] * tile_size * n_cols
    own_u, own_v = u_unit.shape[0], v_unit.shape[0]
    wide = v_unit.shape[2]
    rhs = own_v * n_row
    lanes = -(-rhs // 128) * 128
    block = 2 * own_v
    vmem = 8 + rhs // 16
    first = [1, *range(n_row - 1, 1, -1)]
    second = [*range(2, n_row), 1]
    live, scalars = call(
        prepare_kernel,
        [((u_bases.shape[1], u_bases.shape[3]), f32), ((3, rhs), f32)],
        tile_ranks,
        alpha_prev[None],
        rhobar_prev[None],
        phibar_prev[None],
        cost=pl.CostEstimate(flops=10**10, bytes_accessed=2**26, transcendentals=0),
    )
    first = [1, *range(n_row - 1, 1, -1)]
    second = [*range(2, n_row), 1]
    scalars = jnp.stack([alpha_prev, rhobar_prev, phibar_prev])
    v_low = jnp.swapaxes(v_unit, 0, 1).reshape(block, wide).astype(bf16)
    blocks = [v_low] + [flip(v_low, "row", k) for k in first]
    low, own, kept = call(
        partial(forward_kernel, n_row, first, own_v, own_u),
        [((2 * rhs, tile_size), bf16), ((2 * own_u, tile_size), f32), ((2, block, wide), bf16)],
        live,
        u_bases,
        v_bases,
        u_unit,
        scalars,
        *blocks,
        scratch=[pltpu.VMEM((2 * rhs, tile_size), f32)],
        vmem=vmem,
    )
    got = [flip(low, "cplx", 1)]
    mask = n_cplx
    while mask < n_cols:
        low = (low.astype(f32) + got[-1].astype(f32)).astype(bf16)
        got.append(flip(low, ("col", "cplx"), mask + 1))
        mask *= 2
    *outs, own = call(
        partial(adjoint_kernel, n_row, len(got), own_v, own_u, lanes),
        [((2 * block * (wide // lanes) + 16, lanes), bf16)] * n_row + [((2 * own_u, tile_size), f32)],
        live,
        u_bases,
        v_bases,
        own,
        low,
        *got,
        vmem=vmem,
    )
    sums = [outs[0]] + [flip(outs[k], "row", k) for k in second]
    residual_v, beta, norms = call(
        partial(residual_kernel, n_row, second, rows_total, cols_total, lanes),
        [((block, wide), f32), ((1, lanes), f32), ((1, lanes), f32)],
        v_unit,
        kept,
        *sums,
    )
    norms = norms + flip(norms, "cplx", 1)
    mask = n_cplx
    while 2 * mask < n_cols:
        norms = norms + flip(norms, ("col", "cplx"), mask + 1)
        mask *= 2
    across = [mask] + [k * n_cols + m for k in range(1, n_row // 2) for m in (0, mask)]
    got = [flip(norms, ("row", "col", "cplx"), m + 1) for m in across]
    x_next, w_next, u_next, v_next, norms = call(
        partial(vectors_kernel, cols_total),
        [(x_solution.shape, f32), (w_direction.shape, f32), (u_unit.shape, f32), (v_unit.shape, f32), ((1, lanes), f32)],
        norms,
        got[0],
        beta,
        residual_v,
        own,
        x_solution,
        w_direction,
        scalars,
        cost=pl.CostEstimate(flops=10**9, bytes_accessed=2**23, transcendentals=0),
    )
    alpha, rhobar, phibar = call(
        partial(scalars_kernel, cols_total), [((1, rhs), f32)] * 3, beta, scalars, norms, *third_of(got[1:])
    )
    return (x_next, w_next, u_next, v_next, alpha[0], rhobar[0], phibar[0])


def solution(mesh):
    placed = (
        P(("freq", "row"), ("col", "cplx"), None, None, None),
        P(("freq", "row"), ("col", "cplx"), None, None, None),
        P(("freq", "row"), ("col", "cplx")),
        P(("freq", "col", "cplx"), None, "row"),
        P(("freq", "row"), None, ("col", "cplx")),
        P(("freq", "row"), None, ("col", "cplx")),
        P(("freq", "row"), None, ("col", "cplx")),
        P("freq"),
        P("freq"),
        P("freq"),
    )
    return jax.shard_map(
        body,
        mesh=mesh,
        in_specs=placed,
        out_specs=(
            P(("freq", "row"), None, ("col", "cplx")),
            P(("freq", "row"), None, ("col", "cplx")),
            P(("freq", "col", "cplx"), None, "row"),
            P(("freq", "row"), None, ("col", "cplx")),
            P("freq"),
            P("freq"),
            P("freq"),
        ),
        check_vma=False,
    )
```

```python
from functools import partial

import jax
import jax.numpy as jnp
from jax import lax
from jax.experimental import pallas as pl
from jax.experimental.pallas import tpu as pltpu
from jax.sharding import PartitionSpec as P

epsilon = 1e-06
shrink = 2.0**-20
f32 = jnp.float32
bf16 = jnp.bfloat16


def call(kernel, outs, *args, scratch=(), vmem=12, cost=None):
    in_specs = [pl.BlockSpec(memory_space=pltpu.VMEM)] * len(args)
    return pl.pallas_call(
        kernel,
        out_shape=[jax.ShapeDtypeStruct(s, d) for s, d in outs],
        in_specs=in_specs,
        out_specs=[pl.BlockSpec(memory_space=pltpu.VMEM)] * len(outs),
        scratch_shapes=list(scratch),
        compiler_params=pltpu.CompilerParams(vmem_limit_bytes=vmem * 2**20),
        cost_estimate=cost,
    )(*args)


def iota(shape, dim):
    return lax.broadcasted_iota(jnp.int32, shape, dim)


def to_lanes(column, place, lanes):
    rows = column.shape[0]
    here = iota((rows, lanes), 1) == place
    return jnp.sum(jnp.where(here, column, 0.0), axis=0, keepdims=True)


def to_column(lane_values, first, rows):
    lanes = lane_values.shape[1]
    here = iota((rows, lanes), 1) == iota((rows, lanes), 0) + first
    return jnp.sum(jnp.where(here, lane_values, 0.0), axis=1, keepdims=True)


def dot(a, b, transposed):
    return lax.dot_general(a, b, (((1,), (1 if transposed else 0,)), ((), ())), preferred_element_type=f32)


def through(inner, outer, live_ref, x, own):
    tiles, _, ranks, size = inner.shape[1:]
    mids = []
    gs = [dot(x(q), inner[0, q].reshape(2 * ranks, size), True) for q in range(tiles)]
    for q, g in enumerate(gs):
        rows = g.shape[0]
        g = g.reshape(rows // (2 * own), 2, own, 2 * ranks)
        live = live_ref[q : q + 1, :]
        re = (g[:, 0, :, :ranks] + g[:, 1, :, ranks:]) * live
        im = (g[:, 1, :, :ranks] - g[:, 0, :, ranks:]) * live
        both = jnp.stack([jnp.concatenate([re, -im], 2), jnp.concatenate([im, re], 2)], 1)
        mids.append(both.reshape(rows, 2 * ranks).astype(bf16))
    return [dot(both, outer[0, q].reshape(2 * ranks, size), False) for q, both in enumerate(mids)]


def in_order(blocks, order):
    return [blocks[0]] + [blocks[1 + order.index(k)] for k in range(1, len(blocks))]


def prepare_kernel(ranks_ref, alpha_ref, rhobar_ref, phibar_ref, live_ref, scalars_ref):
    for q in range(live_ref.shape[0]):
        here = iota((1, live_ref.shape[1]), 1) < ranks_ref[0:1, q : q + 1]
        live_ref[q : q + 1, :] = here.astype(f32)
    for i, ref in enumerate((alpha_ref, rhobar_ref, phibar_ref)):
        scalars_ref[i : i + 1, :] = ref[...]


def forward_kernel(n_row, order, own_v, own_u, live_ref, u_bases, v_bases, u_ref, alpha_ref, *refs):
    blocks, (low_ref, own_ref, kept_ref, total) = in_order(refs[:n_row], order), refs[n_row:]
    p, c = lax.axis_index("row"), lax.axis_index(("col", "cplx"))
    size = v_bases.shape[4]
    x = jnp.concatenate([b[...] for b in blocks], 0)
    kept_ref[0] = blocks[0][...]
    kept_ref[1] = blocks[n_row // 2][...]
    parts = through(v_bases, u_bases, live_ref, lambda q: x[:, q * size : (q + 1) * size], own_v)
    total[...] = sum(parts[1:], parts[0])
    many = own_u // own_v
    for b in range(many):
        at = pl.ds(pl.multiple_of(((c * many + b) ^ p) * 2 * own_v, 2 * own_v), 2 * own_v)
        alpha = to_column(alpha_ref[0:1, :], c * own_u + b * own_v, own_v)
        mine = slice(b * own_v, (b + 1) * own_v)
        shift = jnp.concatenate([alpha * u_ref[mine, 0, :], alpha * u_ref[mine, 1, :]], 0)
        left = total[at, :] - shift
        own_ref[b * 2 * own_v : (b + 1) * 2 * own_v, :] = left
        total[at, :] = left
    low_ref[...] = total[...].astype(bf16)


def adjoint_kernel(n_row, n_got, own_v, own_u, lanes, live_ref, u_bases, v_bases, own_ref, sum_ref, *refs):
    got, outs, own_out = refs[:n_got], refs[n_got : n_got + n_row], refs[n_got + n_row]
    p, c = lax.axis_index("row"), lax.axis_index(("col", "cplx"))
    many = own_u // own_v
    for b in range(many):
        at = pl.ds(pl.multiple_of(((c * many + b) ^ p) * 2 * own_v, 2 * own_v), 2 * own_v)
        mine = slice(b * 2 * own_v, (b + 1) * 2 * own_v)
        acc = own_ref[mine, :]
        for g in got:
            acc = acc + g[at, :].astype(f32)
        own_out[mine, :] = acc
    res = sum_ref[...].astype(f32) + got[-1][...].astype(f32)
    rows = res.shape[0]
    squares = jnp.sum(res * res, axis=1, keepdims=True)
    row = iota((rows, 1), 0)
    place = ((row // (2 * own_v)) ^ p) * own_v + row % own_v
    beta2 = to_lanes(squares, place, lanes)
    high = beta2.astype(bf16)
    low = (beta2 - high.astype(f32)).astype(bf16)
    tail = jnp.where(iota((16, lanes), 0) == 0, high.astype(f32), low.astype(f32)).astype(bf16)
    x = (res * shrink).astype(bf16)
    parts = through(u_bases, v_bases, live_ref, lambda q: x, own_v)
    wide = jnp.concatenate(parts, 1).astype(bf16)
    strips = wide.shape[1] // lanes
    for k, out in enumerate(outs):
        for i, j in enumerate((k, k ^ (n_row // 2))):
            for t in range(strips):
                at = (i * strips + t) * 2 * own_v
                out[at : at + 2 * own_v, :] = wide[j * 2 * own_v : (j + 1) * 2 * own_v, t * lanes : (t + 1) * lanes]
        out[2 * strips * 2 * own_v :, :] = tail


def pairs(values):
    while len(values) > 1:
        values = [a + b for a, b in zip(values[::2], values[1::2])]
    return values[0]


def residual_kernel(n_row, order, rows_total, cols_total, lanes, v_ref, kept_ref, *refs):
    blocks, (res_ref, beta_ref, norm_ref) = in_order(refs[:n_row], order), refs[n_row:]
    p = lax.axis_index("row")
    own_v, _, wide = v_ref.shape
    strips = wide // lanes
    end = 2 * strips * 2 * own_v
    beta2 = pairs([b[end : end + 1, :].astype(f32) + b[end + 1 : end + 2, :].astype(f32) for b in blocks])
    beta = jnp.sqrt(beta2 / (2 * rows_total) + epsilon)
    beta_ref[...] = beta
    norms = jnp.zeros((1, lanes), f32)
    for h, row in enumerate((p, p ^ (n_row // 2))):
        beta_here = to_column(beta, row * own_v, own_v)
        beta_here = jnp.concatenate([beta_here, beta_here], 0)
        scale = rows_total / cols_total / shrink / beta_here
        squares = jnp.zeros((own_v, lanes), f32)
        for t in range(strips):
            at = (h * strips + t) * 2 * own_v
            back = scale * pairs([b[at : at + 2 * own_v, :].astype(f32) for b in blocks])
            strip = slice(t * lanes, (t + 1) * lanes)
            low = beta_here * kept_ref[h, :, strip].astype(f32)
            for i in range(2):
                half = slice(i * own_v, (i + 1) * own_v)
                if h == 0:
                    res_ref[half, strip] = back[half] - beta_here[half] * v_ref[:, i, strip]
                res = back[half] - low[half]
                squares = squares + res * res
        squares = jnp.sum(squares, axis=1, keepdims=True)
        place = iota((own_v, 1), 0) + row * own_v
        norms = norms + to_lanes(squares, place, lanes)
    norm_ref[...] = norms


def turn(beta, scalars_ref):
    rhobar, phibar = scalars_ref[1:2, :], scalars_ref[2:3, :]
    rho = jnp.sqrt(rhobar * rhobar + beta * beta)
    return rho, rhobar / rho, beta / rho, phibar


def vectors_kernel(cols_total, norms_ref, got_ref, beta_ref, res_ref, own_ref, x_ref, w_ref, scalars_ref, x_out, w_out, u_out, v_out, sum_out):
    p, c = lax.axis_index("row"), lax.axis_index(("col", "cplx"))
    own_v = x_ref.shape[0]
    own_u = u_out.shape[0]
    many = own_u // own_v
    rhs = scalars_ref.shape[1]
    beta = beta_ref[:, :rhs]
    rho, cosine, sine, phibar = turn(beta, scalars_ref)
    norms = norms_ref[...] + got_ref[...]
    sum_out[...] = norms
    alpha2 = to_column(norms, p * own_v, own_v)
    alpha = jnp.sqrt(alpha2 / (2 * cols_total) + epsilon)
    step_x = to_column(cosine * phibar / rho, p * own_v, own_v)
    step_w = to_column(sine / rho, p * own_v, own_v) * alpha
    for i in range(2):
        w = w_ref[:, i, :]
        v = res_ref[i * own_v : (i + 1) * own_v, :] / alpha
        x_out[:, i, :] = x_ref[:, i, :] + step_x * w
        v_out[:, i, :] = v
        w_out[:, i, :] = v - step_w * w
    for b in range(many):
        beta_own = to_column(beta, c * own_u + b * own_v, own_v)
        for i in range(2):
            u = own_ref[(2 * b + i) * own_v : (2 * b + i + 1) * own_v, :]
            u_out[b * own_v : (b + 1) * own_v, i, :] = u / beta_own


def scalars_kernel(cols_total, beta_ref, scalars_ref, *refs):
    norms, (alpha_out, rhobar_out, phibar_out) = refs[:-3], refs[-3:]
    rhs = scalars_ref.shape[1]
    rho, cosine, sine, phibar = turn(beta_ref[:, :rhs], scalars_ref)
    alpha2 = sum([n[...] for n in norms[1:]], norms[0][...])[:, :rhs]
    alpha = jnp.sqrt(alpha2 / (2 * cols_total) + epsilon)
    alpha_out[...] = alpha
    rhobar_out[...] = -cosine * alpha
    phibar_out[...] = sine * phibar


def third_of(x):
    return x


def flip(x, axes, mask):
    return lax.ppermute(x, axes, [(i, i ^ mask) for i in range(lax.axis_size(axes))])


def body(
    u_bases,
    v_bases,
    tile_ranks,
    u_unit,
    v_unit,
    x_solution,
    w_direction,
    alpha_prev,
    rhobar_prev,
    phibar_prev,
):
    tile_size = u_bases.shape[4]
    n_row = lax.axis_size("row")
    n_cplx = lax.axis_size("cplx")
    n_cols = lax.axis_size(("col", "cplx"))
    rows_total = tile_size * n_row
    cols_total = u_bases.shape[1] * tile_size * n_cols
    own_u, own_v = u_unit.shape[0], v_unit.shape[0]
    wide = v_unit.shape[2]
    rhs = own_v * n_row
    lanes = -(-rhs // 128) * 128
    block = 2 * own_v
    vmem = 8 + rhs // 16
    first = [1, *range(n_row - 1, 1, -1)]
    second = [*range(2, n_row), 1]
    live, scalars = call(
        prepare_kernel,
        [((u_bases.shape[1], u_bases.shape[3]), f32), ((3, rhs), f32)],
        tile_ranks,
        alpha_prev[None],
        rhobar_prev[None],
        phibar_prev[None],
        cost=pl.CostEstimate(flops=10**10, bytes_accessed=2**26, transcendentals=0),
    )
    first = [1, *range(n_row - 1, 1, -1)]
    second = [*range(2, n_row), 1]
    scalars = jnp.stack([alpha_prev, rhobar_prev, phibar_prev])
    v_low = jnp.swapaxes(v_unit, 0, 1).reshape(block, wide).astype(bf16)
    blocks = [v_low] + [flip(v_low, "row", k) for k in first]
    low, own, kept = call(
        partial(forward_kernel, n_row, first, own_v, own_u),
        [((2 * rhs, tile_size), bf16), ((2 * own_u, tile_size), f32), ((2, block, wide), bf16)],
        live,
        u_bases,
        v_bases,
        u_unit,
        scalars,
        *blocks,
        scratch=[pltpu.VMEM((2 * rhs, tile_size), f32)],
        vmem=vmem,
    )
    got = [flip(low, "cplx", 1)]
    mask = n_cplx
    while mask < n_cols:
        low = (low.astype(f32) + got[-1].astype(f32)).astype(bf16)
        got.append(flip(low, ("col", "cplx"), mask))
        mask *= 2
    *outs, own = call(
        partial(adjoint_kernel, n_row, len(got), own_v, own_u, lanes),
        [((2 * block * (wide // lanes) + 16, lanes), bf16)] * n_row + [((2 * own_u, tile_size), f32)],
        live,
        u_bases,
        v_bases,
        own,
        low,
        *got,
        vmem=vmem,
    )
    sums = [outs[0]] + [flip(outs[k], "row", k) for k in second]
    residual_v, beta, norms = call(
        partial(residual_kernel, n_row, second, rows_total, cols_total, lanes),
        [((block, wide), f32), ((1, lanes), f32), ((1, lanes), f32)],
        v_unit,
        kept,
        *sums,
    )
    norms = norms + flip(norms, "cplx", 1)
    mask = n_cplx
    while 2 * mask < n_cols:
        norms = norms + flip(norms, ("col", "cplx"), mask + 1)
        mask *= 2
    across = [mask] + [k * n_cols + m for k in range(1, n_row // 2) for m in (0, mask)]
    got = [flip(norms, ("row", "col", "cplx"), m + 1) for m in across]
    x_next, w_next, u_next, v_next, norms = call(
        partial(vectors_kernel, cols_total),
        [(x_solution.shape, f32), (w_direction.shape, f32), (u_unit.shape, f32), (v_unit.shape, f32), ((1, lanes), f32)],
        norms,
        got[0],
        beta,
        residual_v,
        own,
        x_solution,
        w_direction,
        scalars,
        cost=pl.CostEstimate(flops=10**9, bytes_accessed=2**23, transcendentals=0),
    )
    alpha, rhobar, phibar = call(
        partial(scalars_kernel, cols_total), [((1, rhs), f32)] * 3, beta, scalars, norms, *third_of(got[1:])
    )
    return (x_next, w_next, u_next, v_next, alpha[0], rhobar[0], phibar[0])


def solution(mesh):
    placed = (
        P(("freq", "row"), ("col", "cplx"), None, None, None),
        P(("freq", "row"), ("col", "cplx"), None, None, None),
        P(("freq", "row"), ("col", "cplx")),
        P(("freq", "col", "cplx"), None, "row"),
        P(("freq", "row"), None, ("col", "cplx")),
        P(("freq", "row"), None, ("col", "cplx")),
        P(("freq", "row"), None, ("col", "cplx")),
        P("freq"),
        P("freq"),
        P("freq"),
    )
    return jax.shard_map(
        body,
        mesh=mesh,
        in_specs=placed,
        out_specs=(
            P(("freq", "row"), None, ("col", "cplx")),
            P(("freq", "row"), None, ("col", "cplx")),
            P(("freq", "col", "cplx"), None, "row"),
            P(("freq", "row"), None, ("col", "cplx")),
            P("freq"),
            P("freq"),
            P("freq"),
        ),
        check_vma=False,
    )
```

```python
from functools import partial

import jax
import jax.numpy as jnp
from jax import lax
from jax.experimental import pallas as pl
from jax.experimental.pallas import tpu as pltpu
from jax.sharding import PartitionSpec as P

epsilon = 1e-06
shrink = 2.0**-20
f32 = jnp.float32
bf16 = jnp.bfloat16


def call(kernel, outs, *args, scratch=(), vmem=12, cost=None):
    in_specs = [pl.BlockSpec(memory_space=pltpu.VMEM)] * len(args)
    return pl.pallas_call(
        kernel,
        out_shape=[jax.ShapeDtypeStruct(s, d) for s, d in outs],
        in_specs=in_specs,
        out_specs=[pl.BlockSpec(memory_space=pltpu.VMEM)] * len(outs),
        scratch_shapes=list(scratch),
        compiler_params=pltpu.CompilerParams(vmem_limit_bytes=vmem * 2**20),
        cost_estimate=cost,
    )(*args)


def iota(shape, dim):
    return lax.broadcasted_iota(jnp.int32, shape, dim)


def to_lanes(column, place, lanes):
    rows = column.shape[0]
    here = iota((rows, lanes), 1) == place
    return jnp.sum(jnp.where(here, column, 0.0), axis=0, keepdims=True)


def to_column(lane_values, first, rows):
    lanes = lane_values.shape[1]
    here = iota((rows, lanes), 1) == iota((rows, lanes), 0) + first
    return jnp.sum(jnp.where(here, lane_values, 0.0), axis=1, keepdims=True)


def dot(a, b, transposed):
    return lax.dot_general(a, b, (((1,), (1 if transposed else 0,)), ((), ())), preferred_element_type=f32)


def through(inner, outer, live_ref, x, own):
    tiles, _, ranks, size = inner.shape[1:]
    mids = []
    gs = [dot(x(q), inner[0, q].reshape(2 * ranks, size), True) for q in range(tiles)]
    for q, g in enumerate(gs):
        rows = g.shape[0]
        g = g.reshape(rows // (2 * own), 2, own, 2 * ranks)
        live = live_ref[q : q + 1, :]
        re = (g[:, 0, :, :ranks] + g[:, 1, :, ranks:]) * live
        im = (g[:, 1, :, :ranks] - g[:, 0, :, ranks:]) * live
        both = jnp.stack([jnp.concatenate([re, -im], 2), jnp.concatenate([im, re], 2)], 1)
        mids.append(both.reshape(rows, 2 * ranks).astype(bf16))
    return [dot(both, outer[0, q].reshape(2 * ranks, size), False) for q, both in enumerate(mids)]


def in_order(blocks, order):
    return [blocks[0]] + [blocks[1 + order.index(k)] for k in range(1, len(blocks))]


def prepare_kernel(ranks_ref, alpha_ref, rhobar_ref, phibar_ref, live_ref, scalars_ref):
    for q in range(live_ref.shape[0]):
        here = iota((1, live_ref.shape[1]), 1) < ranks_ref[0:1, q : q + 1]
        live_ref[q : q + 1, :] = here.astype(f32)
    for i, ref in enumerate((alpha_ref, rhobar_ref, phibar_ref)):
        scalars_ref[i : i + 1, :] = ref[...]


def forward_kernel(n_row, order, own_v, own_u, live_ref, u_bases, v_bases, u_ref, alpha_ref, *refs):
    blocks, (low_ref, own_ref, kept_ref, total) = in_order(refs[:n_row], order), refs[n_row:]
    p, c = lax.axis_index("row"), lax.axis_index(("col", "cplx"))
    size = v_bases.shape[4]
    x = jnp.concatenate([b[...] for b in blocks], 0)
    kept_ref[0] = blocks[0][...]
    kept_ref[1] = blocks[n_row // 2][...]
    parts = through(v_bases, u_bases, live_ref, lambda q: x[:, q * size : (q + 1) * size], own_v)
    total[...] = sum(parts[1:], parts[0])
    many = own_u // own_v
    for b in range(many):
        at = pl.ds(pl.multiple_of(((c * many + b) ^ p) * 2 * own_v, 2 * own_v), 2 * own_v)
        alpha = to_column(alpha_ref[0:1, :], c * own_u + b * own_v, own_v)
        mine = slice(b * own_v, (b + 1) * own_v)
        shift = jnp.concatenate([alpha * u_ref[mine, 0, :], alpha * u_ref[mine, 1, :]], 0)
        left = total[at, :] - shift
        own_ref[b * 2 * own_v : (b + 1) * 2 * own_v, :] = left
        total[at, :] = left
    low_ref[...] = total[...].astype(bf16)


def adjoint_kernel(n_row, n_got, own_v, own_u, lanes, live_ref, u_bases, v_bases, own_ref, sum_ref, *refs):
    got, outs, own_out = refs[:n_got], refs[n_got : n_got + n_row], refs[n_got + n_row]
    p, c = lax.axis_index("row"), lax.axis_index(("col", "cplx"))
    many = own_u // own_v
    for b in range(many):
        at = pl.ds(pl.multiple_of(((c * many + b) ^ p) * 2 * own_v, 2 * own_v), 2 * own_v)
        mine = slice(b * 2 * own_v, (b + 1) * 2 * own_v)
        acc = own_ref[mine, :]
        for g in got:
            acc = acc + g[at, :].astype(f32)
        own_out[mine, :] = acc
    res = sum_ref[...].astype(f32) + got[-1][...].astype(f32)
    rows = res.shape[0]
    squares = jnp.sum(res * res, axis=1, keepdims=True)
    row = iota((rows, 1), 0)
    place = ((row // (2 * own_v)) ^ p) * own_v + row % own_v
    beta2 = to_lanes(squares, place, lanes)
    high = beta2.astype(bf16)
    low = (beta2 - high.astype(f32)).astype(bf16)
    tail = jnp.where(iota((16, lanes), 0) == 0, high.astype(f32), low.astype(f32)).astype(bf16)
    x = (res * shrink).astype(bf16)
    parts = through(u_bases, v_bases, live_ref, lambda q: x, own_v)
    wide = jnp.concatenate(parts, 1).astype(bf16)
    strips = wide.shape[1] // lanes
    for k, out in enumerate(outs):
        for i, j in enumerate((k, k ^ (n_row // 2))):
            for t in range(strips):
                at = (i * strips + t) * 2 * own_v
                out[at : at + 2 * own_v, :] = wide[j * 2 * own_v : (j + 1) * 2 * own_v, t * lanes : (t + 1) * lanes]
        out[2 * strips * 2 * own_v :, :] = tail


def pairs(values):
    while len(values) > 1:
        values = [a + b for a, b in zip(values[::2], values[1::2])]
    return values[0]


def residual_kernel(n_row, order, rows_total, cols_total, lanes, v_ref, kept_ref, *refs):
    blocks, (res_ref, beta_ref, norm_ref) = in_order(refs[:n_row], order), refs[n_row:]
    p = lax.axis_index("row")
    own_v, _, wide = v_ref.shape
    strips = wide // lanes
    end = 2 * strips * 2 * own_v
    beta2 = pairs([b[end : end + 1, :].astype(f32) + b[end + 1 : end + 2, :].astype(f32) for b in blocks])
    beta = jnp.sqrt(beta2 / (2 * rows_total) + epsilon)
    beta_ref[...] = beta
    rows = (p, p ^ (n_row // 2))
    first = jnp.where(iota((4 * own_v, 1), 0) < 2 * own_v, rows[0], rows[1]) * own_v + iota((4 * own_v, 1), 0) % own_v
    here = iota((4 * own_v, lanes), 1) == first
    betas = jnp.sum(jnp.where(here, beta, 0.0), axis=1, keepdims=True)
    scales = rows_total / cols_total / shrink / betas
    squares = []
    for h in range(2):
        both = slice(h * 2 * own_v, (h + 1) * 2 * own_v)
        beta_here, scale = betas[both], scales[both]
        total = jnp.zeros((2 * own_v, lanes), f32)
        for t in range(strips):
            at = (h * strips + t) * 2 * own_v
            back = scale * pairs([b[at : at + 2 * own_v, :].astype(f32) for b in blocks])
            strip = slice(t * lanes, (t + 1) * lanes)
            if h == 0:
                for i in range(2):
                    half = slice(i * own_v, (i + 1) * own_v)
                    res_ref[half, strip] = back[half] - beta_here[half] * v_ref[:, i, strip]
            res = back - beta_here * kept_ref[h, :, strip].astype(f32)
            total = total + res * res
        squares.append(total)
    squares = jnp.sum(jnp.concatenate(squares, 0), axis=1, keepdims=True)
    norm_ref[...] = jnp.sum(jnp.where(here, squares, 0.0), axis=0, keepdims=True)


def turn(beta, scalars_ref):
    rhobar, phibar = scalars_ref[1:2, :], scalars_ref[2:3, :]
    rho = jnp.sqrt(rhobar * rhobar + beta * beta)
    return rho, rhobar / rho, beta / rho, phibar


def vectors_kernel(cols_total, norms_ref, got_ref, beta_ref, res_ref, own_ref, x_ref, w_ref, scalars_ref, x_out, w_out, u_out, v_out, sum_out):
    p, c = lax.axis_index("row"), lax.axis_index(("col", "cplx"))
    own_v = x_ref.shape[0]
    own_u = u_out.shape[0]
    many = own_u // own_v
    rhs = scalars_ref.shape[1]
    beta = beta_ref[:, :rhs]
    rho, cosine, sine, phibar = turn(beta, scalars_ref)
    norms = norms_ref[...] + got_ref[...]
    sum_out[...] = norms
    alpha2 = to_column(norms, p * own_v, own_v)
    alpha = jnp.sqrt(alpha2 / (2 * cols_total) + epsilon)
    step_x = to_column(cosine * phibar / rho, p * own_v, own_v)
    step_w = to_column(sine / rho, p * own_v, own_v) * alpha
    for i in range(2):
        w = w_ref[:, i, :]
        v = res_ref[i * own_v : (i + 1) * own_v, :] / alpha
        x_out[:, i, :] = x_ref[:, i, :] + step_x * w
        v_out[:, i, :] = v
        w_out[:, i, :] = v - step_w * w
    for b in range(many):
        beta_own = to_column(beta, c * own_u + b * own_v, own_v)
        for i in range(2):
            u = own_ref[(2 * b + i) * own_v : (2 * b + i + 1) * own_v, :]
            u_out[b * own_v : (b + 1) * own_v, i, :] = u / beta_own


def scalars_kernel(cols_total, beta_ref, scalars_ref, *refs):
    norms, (alpha_out, rhobar_out, phibar_out) = refs[:-3], refs[-3:]
    rhs = scalars_ref.shape[1]
    rho, cosine, sine, phibar = turn(beta_ref[:, :rhs], scalars_ref)
    alpha2 = sum([n[...] for n in norms[1:]], norms[0][...])[:, :rhs]
    alpha = jnp.sqrt(alpha2 / (2 * cols_total) + epsilon)
    alpha_out[...] = alpha
    rhobar_out[...] = -cosine * alpha
    phibar_out[...] = sine * phibar


def flip(x, axes, mask):
    return lax.ppermute(x, axes, [(i, i ^ mask) for i in range(lax.axis_size(axes))])


def body(
    u_bases,
    v_bases,
    tile_ranks,
    u_unit,
    v_unit,
    x_solution,
    w_direction,
    alpha_prev,
    rhobar_prev,
    phibar_prev,
):
    tile_size = u_bases.shape[4]
    n_row = lax.axis_size("row")
    n_cplx = lax.axis_size("cplx")
    n_cols = lax.axis_size(("col", "cplx"))
    rows_total = tile_size * n_row
    cols_total = u_bases.shape[1] * tile_size * n_cols
    own_u, own_v = u_unit.shape[0], v_unit.shape[0]
    wide = v_unit.shape[2]
    rhs = own_v * n_row
    lanes = -(-rhs // 128) * 128
    block = 2 * own_v
    vmem = 8 + rhs // 16
    first = [1, *range(n_row - 1, 1, -1)]
    second = [*range(2, n_row), 1]
    live, scalars = call(
        prepare_kernel,
        [((u_bases.shape[1], u_bases.shape[3]), f32), ((3, rhs), f32)],
        tile_ranks,
        alpha_prev[None],
        rhobar_prev[None],
        phibar_prev[None],
        cost=pl.CostEstimate(flops=10**10, bytes_accessed=2**26, transcendentals=0),
    )
    first = [1, *range(n_row - 1, 1, -1)]
    second = [*range(2, n_row), 1]
    v_low = jnp.swapaxes(v_unit, 0, 1).reshape(block, wide).astype(bf16)
    blocks = [v_low] + [flip(v_low, "row", k) for k in first]
    low, own, kept = call(
        partial(forward_kernel, n_row, first, own_v, own_u),
        [((2 * rhs, tile_size), bf16), ((2 * own_u, tile_size), f32), ((2, block, wide), bf16)],
        live,
        u_bases,
        v_bases,
        u_unit,
        scalars,
        *blocks,
        scratch=[pltpu.VMEM((2 * rhs, tile_size), f32)],
        vmem=vmem,
    )
    got = [flip(low, "cplx", 1)]
    mask = n_cplx
    while mask < n_cols:
        low = (low.astype(f32) + got[-1].astype(f32)).astype(bf16)
        got.append(flip(low, ("col", "cplx"), mask))
        mask *= 2
    *outs, own = call(
        partial(adjoint_kernel, n_row, len(got), own_v, own_u, lanes),
        [((2 * block * (wide // lanes) + 16, lanes), bf16)] * n_row + [((2 * own_u, tile_size), f32)],
        live,
        u_bases,
        v_bases,
        own,
        low,
        *got,
        vmem=vmem,
    )
    sums = [outs[0]] + [flip(outs[k], "row", k) for k in second]
    residual_v, beta, norms = call(
        partial(residual_kernel, n_row, second, rows_total, cols_total, lanes),
        [((block, wide), f32), ((1, lanes), f32), ((1, lanes), f32)],
        v_unit,
        kept,
        *sums,
    )
    norms = norms + flip(norms, "cplx", 1)
    mask = n_cplx
    while 2 * mask < n_cols:
        norms = norms + flip(norms, ("col", "cplx"), mask + 1)
        mask *= 2
    across = [mask] + [k * n_cols + m for k in range(1, n_row // 2) for m in (0, mask)]
    got = [flip(norms, ("row", "col", "cplx"), m + 1) for m in across]
    x_next, w_next, u_next, v_next, norms = call(
        partial(vectors_kernel, cols_total),
        [(x_solution.shape, f32), (w_direction.shape, f32), (u_unit.shape, f32), (v_unit.shape, f32), ((1, lanes), f32)],
        norms,
        got[0],
        beta,
        residual_v,
        own,
        x_solution,
        w_direction,
        scalars,
        cost=pl.CostEstimate(flops=10**9, bytes_accessed=2**23, transcendentals=0),
    )
    alpha, rhobar, phibar = call(
        partial(scalars_kernel, cols_total), [((1, rhs), f32)] * 3, beta, scalars, norms, *got[1:]
    )
    return (x_next, w_next, u_next, v_next, alpha[0], rhobar[0], phibar[0])


def solution(mesh):
    placed = (
        P(("freq", "row"), ("col", "cplx"), None, None, None),
        P(("freq", "row"), ("col", "cplx"), None, None, None),
        P(("freq", "row"), ("col", "cplx")),
        P(("freq", "col", "cplx"), None, "row"),
        P(("freq", "row"), None, ("col", "cplx")),
        P(("freq", "row"), None, ("col", "cplx")),
        P(("freq", "row"), None, ("col", "cplx")),
        P("freq"),
        P("freq"),
        P("freq"),
    )
    return jax.shard_map(
        body,
        mesh=mesh,
        in_specs=placed,
        out_specs=(
            P(("freq", "row"), None, ("col", "cplx")),
            P(("freq", "row"), None, ("col", "cplx")),
            P(("freq", "col", "cplx"), None, "row"),
            P(("freq", "row"), None, ("col", "cplx")),
            P("freq"),
            P("freq"),
            P("freq"),
        ),
        check_vma=False,
    )
```

```python
from functools import partial

import jax
import jax.numpy as jnp
from jax import lax
from jax.experimental import pallas as pl
from jax.experimental.pallas import tpu as pltpu
from jax.sharding import PartitionSpec as P

epsilon = 1e-06
shrink = 2.0**-20
f32 = jnp.float32
bf16 = jnp.bfloat16


def call(kernel, outs, *args, scratch=(), vmem=12, cost=None):
    in_specs = [pl.BlockSpec(memory_space=pltpu.VMEM)] * len(args)
    return pl.pallas_call(
        kernel,
        out_shape=[jax.ShapeDtypeStruct(s, d) for s, d in outs],
        in_specs=in_specs,
        out_specs=[pl.BlockSpec(memory_space=pltpu.VMEM)] * len(outs),
        scratch_shapes=list(scratch),
        compiler_params=pltpu.CompilerParams(vmem_limit_bytes=vmem * 2**20),
        cost_estimate=cost,
    )(*args)


def iota(shape, dim):
    return lax.broadcasted_iota(jnp.int32, shape, dim)


def to_lanes(column, place, lanes):
    rows = column.shape[0]
    here = iota((rows, lanes), 1) == place
    return jnp.sum(jnp.where(here, column, 0.0), axis=0, keepdims=True)


def to_column(lane_values, first, rows):
    lanes = lane_values.shape[1]
    here = iota((rows, lanes), 1) == iota((rows, lanes), 0) + first
    return jnp.sum(jnp.where(here, lane_values, 0.0), axis=1, keepdims=True)


def dot(a, b, transposed):
    return lax.dot_general(a, b, (((1,), (1 if transposed else 0,)), ((), ())), preferred_element_type=f32)


def through(inner, outer, live_ref, x, own):
    tiles, _, ranks, size = outer.shape[1:]
    mids = []
    if len(inner.shape) == 3:
        gs = [dot(x(q), inner[q], False) for q in range(tiles)]
    else:
        gs = [dot(x(q), inner[0, q].reshape(2 * ranks, size), True) for q in range(tiles)]
    for q, g in enumerate(gs):
        rows = g.shape[0]
        g = g.reshape(rows // (2 * own), 2, own, 2 * ranks)
        live = live_ref[q : q + 1, :]
        re = (g[:, 0, :, :ranks] + g[:, 1, :, ranks:]) * live
        im = (g[:, 1, :, :ranks] - g[:, 0, :, ranks:]) * live
        both = jnp.stack([jnp.concatenate([re, -im], 2), jnp.concatenate([im, re], 2)], 1)
        mids.append(both.reshape(rows, 2 * ranks).astype(bf16))
    return [dot(both, outer[0, q].reshape(2 * ranks, size), False) for q, both in enumerate(mids)]


def in_order(blocks, order):
    return [blocks[0]] + [blocks[1 + order.index(k)] for k in range(1, len(blocks))]


def prepare_kernel(ranks_ref, alpha_ref, rhobar_ref, phibar_ref, live_ref, scalars_ref):
    for q in range(live_ref.shape[0]):
        here = iota((1, live_ref.shape[1]), 1) < ranks_ref[0:1, q : q + 1]
        live_ref[q : q + 1, :] = here.astype(f32)
    for i, ref in enumerate((alpha_ref, rhobar_ref, phibar_ref)):
        scalars_ref[i : i + 1, :] = ref[...]


def forward_kernel(n_row, order, own_v, own_u, live_ref, u_bases, v_bases, u_ref, alpha_ref, *refs):
    blocks, (low_ref, own_ref, kept_ref, total) = in_order(refs[:n_row], order), refs[n_row:]
    p, c = lax.axis_index("row"), lax.axis_index(("col", "cplx"))
    size = u_bases.shape[4]
    x = jnp.concatenate([b[...] for b in blocks], 0)
    kept_ref[0] = blocks[0][...]
    kept_ref[1] = blocks[n_row // 2][...]
    parts = through(v_bases, u_bases, live_ref, lambda q: x[:, q * size : (q + 1) * size], own_v)
    total[...] = sum(parts[1:], parts[0])
    many = own_u // own_v
    for b in range(many):
        at = pl.ds(pl.multiple_of(((c * many + b) ^ p) * 2 * own_v, 2 * own_v), 2 * own_v)
        alpha = to_column(alpha_ref[0:1, :], c * own_u + b * own_v, own_v)
        mine = slice(b * own_v, (b + 1) * own_v)
        shift = jnp.concatenate([alpha * u_ref[mine, 0, :], alpha * u_ref[mine, 1, :]], 0)
        left = total[at, :] - shift
        own_ref[b * 2 * own_v : (b + 1) * 2 * own_v, :] = left
        total[at, :] = left
    low_ref[...] = total[...].astype(bf16)


def adjoint_kernel(n_row, n_got, own_v, own_u, lanes, live_ref, u_turned, v_bases, own_ref, sum_ref, *refs):
    got, outs, own_out = refs[:n_got], refs[n_got : n_got + n_row], refs[n_got + n_row]
    p, c = lax.axis_index("row"), lax.axis_index(("col", "cplx"))
    many = own_u // own_v
    for b in range(many):
        at = pl.ds(pl.multiple_of(((c * many + b) ^ p) * 2 * own_v, 2 * own_v), 2 * own_v)
        mine = slice(b * 2 * own_v, (b + 1) * 2 * own_v)
        acc = own_ref[mine, :]
        for g in got:
            acc = acc + g[at, :].astype(f32)
        own_out[mine, :] = acc
    res = sum_ref[...].astype(f32) + got[-1][...].astype(f32)
    rows = res.shape[0]
    squares = jnp.sum(res * res, axis=1, keepdims=True)
    row = iota((rows, 1), 0)
    place = ((row // (2 * own_v)) ^ p) * own_v + row % own_v
    beta2 = to_lanes(squares, place, lanes)
    high = beta2.astype(bf16)
    low = (beta2 - high.astype(f32)).astype(bf16)
    tail = jnp.where(iota((16, lanes), 0) == 0, high.astype(f32), low.astype(f32)).astype(bf16)
    x = (res * shrink).astype(bf16)
    parts = through(u_turned, v_bases, live_ref, lambda q: x, own_v)
    wide = jnp.concatenate(parts, 1).astype(bf16)
    strips = wide.shape[1] // lanes
    for k, out in enumerate(outs):
        for i, j in enumerate((k, k ^ (n_row // 2))):
            for t in range(strips):
                at = (i * strips + t) * 2 * own_v
                out[at : at + 2 * own_v, :] = wide[j * 2 * own_v : (j + 1) * 2 * own_v, t * lanes : (t + 1) * lanes]
        out[2 * strips * 2 * own_v :, :] = tail


def pairs(values):
    while len(values) > 1:
        values = [a + b for a, b in zip(values[::2], values[1::2])]
    return values[0]


def residual_kernel(n_row, order, rows_total, cols_total, lanes, v_ref, kept_ref, *refs):
    blocks, (res_ref, beta_ref, norm_ref) = in_order(refs[:n_row], order), refs[n_row:]
    p = lax.axis_index("row")
    own_v, _, wide = v_ref.shape
    strips = wide // lanes
    end = 2 * strips * 2 * own_v
    beta2 = pairs([b[end : end + 1, :].astype(f32) + b[end + 1 : end + 2, :].astype(f32) for b in blocks])
    beta = jnp.sqrt(beta2 / (2 * rows_total) + epsilon)
    beta_ref[...] = beta
    rows = (p, p ^ (n_row // 2))
    first = jnp.where(iota((4 * own_v, 1), 0) < 2 * own_v, rows[0], rows[1]) * own_v + iota((4 * own_v, 1), 0) % own_v
    here = iota((4 * own_v, lanes), 1) == first
    betas = jnp.sum(jnp.where(here, beta, 0.0), axis=1, keepdims=True)
    scales = rows_total / cols_total / shrink / betas
    squares = []
    for h in range(2):
        both = slice(h * 2 * own_v, (h + 1) * 2 * own_v)
        beta_here, scale = betas[both], scales[both]
        total = jnp.zeros((2 * own_v, lanes), f32)
        for t in range(strips):
            at = (h * strips + t) * 2 * own_v
            back = scale * pairs([b[at : at + 2 * own_v, :].astype(f32) for b in blocks])
            strip = slice(t * lanes, (t + 1) * lanes)
            if h == 0:
                for i in range(2):
                    half = slice(i * own_v, (i + 1) * own_v)
                    res_ref[half, strip] = back[half] - beta_here[half] * v_ref[:, i, strip]
            res = back - beta_here * kept_ref[h, :, strip].astype(f32)
            total = total + res * res
        squares.append(total)
    squares = jnp.sum(jnp.concatenate(squares, 0), axis=1, keepdims=True)
    norm_ref[...] = jnp.sum(jnp.where(here, squares, 0.0), axis=0, keepdims=True)


def turn(beta, scalars_ref):
    rhobar, phibar = scalars_ref[1:2, :], scalars_ref[2:3, :]
    rho = jnp.sqrt(rhobar * rhobar + beta * beta)
    return rho, rhobar / rho, beta / rho, phibar


def vectors_kernel(cols_total, norms_ref, got_ref, beta_ref, res_ref, own_ref, x_ref, w_ref, scalars_ref, x_out, w_out, u_out, v_out, sum_out):
    p, c = lax.axis_index("row"), lax.axis_index(("col", "cplx"))
    own_v = x_ref.shape[0]
    own_u = u_out.shape[0]
    many = own_u // own_v
    rhs = scalars_ref.shape[1]
    beta = beta_ref[:, :rhs]
    rho, cosine, sine, phibar = turn(beta, scalars_ref)
    norms = norms_ref[...] + got_ref[...]
    sum_out[...] = norms
    alpha2 = to_column(norms, p * own_v, own_v)
    alpha = jnp.sqrt(alpha2 / (2 * cols_total) + epsilon)
    step_x = to_column(cosine * phibar / rho, p * own_v, own_v)
    step_w = to_column(sine / rho, p * own_v, own_v) * alpha
    for i in range(2):
        w = w_ref[:, i, :]
        v = res_ref[i * own_v : (i + 1) * own_v, :] / alpha
        x_out[:, i, :] = x_ref[:, i, :] + step_x * w
        v_out[:, i, :] = v
        w_out[:, i, :] = v - step_w * w
    for b in range(many):
        beta_own = to_column(beta, c * own_u + b * own_v, own_v)
        for i in range(2):
            u = own_ref[(2 * b + i) * own_v : (2 * b + i + 1) * own_v, :]
            u_out[b * own_v : (b + 1) * own_v, i, :] = u / beta_own


def scalars_kernel(cols_total, beta_ref, scalars_ref, *refs):
    norms, (alpha_out, rhobar_out, phibar_out) = refs[:-3], refs[-3:]
    rhs = scalars_ref.shape[1]
    rho, cosine, sine, phibar = turn(beta_ref[:, :rhs], scalars_ref)
    alpha2 = sum([n[...] for n in norms[1:]], norms[0][...])[:, :rhs]
    alpha = jnp.sqrt(alpha2 / (2 * cols_total) + epsilon)
    alpha_out[...] = alpha
    rhobar_out[...] = -cosine * alpha
    phibar_out[...] = sine * phibar


def flip(x, axes, mask):
    return lax.ppermute(x, axes, [(i, i ^ mask) for i in range(lax.axis_size(axes))])


def body(
    u_bases,
    v_bases,
    tile_ranks,
    u_unit,
    v_unit,
    x_solution,
    w_direction,
    alpha_prev,
    rhobar_prev,
    phibar_prev,
):
    tile_size = u_bases.shape[4]
    n_row = lax.axis_size("row")
    n_cplx = lax.axis_size("cplx")
    n_cols = lax.axis_size(("col", "cplx"))
    rows_total = tile_size * n_row
    cols_total = u_bases.shape[1] * tile_size * n_cols
    own_u, own_v = u_unit.shape[0], v_unit.shape[0]
    wide = v_unit.shape[2]
    rhs = own_v * n_row
    lanes = -(-rhs // 128) * 128
    block = 2 * own_v
    vmem = 8 + rhs // 16
    first = [1, *range(n_row - 1, 1, -1)]
    second = [*range(2, n_row), 1]
    live, scalars = call(
        prepare_kernel,
        [((u_bases.shape[1], u_bases.shape[3]), f32), ((3, rhs), f32)],
        tile_ranks,
        alpha_prev[None],
        rhobar_prev[None],
        phibar_prev[None],
        cost=pl.CostEstimate(flops=10**10, bytes_accessed=2**26, transcendentals=0),
    )
    first = [1, *range(n_row - 1, 1, -1)]
    second = [*range(2, n_row), 1]
    v_low = jnp.swapaxes(v_unit, 0, 1).reshape(block, wide).astype(bf16)
    blocks = [v_low] + [flip(v_low, "row", k) for k in first]
    tiles, _, ranks, size = u_bases.shape[1:]
    u_turned = jnp.swapaxes(u_bases.reshape(tiles, 2 * ranks, size), 1, 2)
    low, own, kept = call(
        partial(forward_kernel, n_row, first, own_v, own_u),
        [((2 * rhs, tile_size), bf16), ((2 * own_u, tile_size), f32), ((2, block, wide), bf16)],
        live,
        u_bases,
        v_bases,
        u_unit,
        scalars,
        *blocks,
        scratch=[pltpu.VMEM((2 * rhs, tile_size), f32)],
        vmem=vmem,
    )
    got = [flip(low, "cplx", 1)]
    mask = n_cplx
    while mask < n_cols:
        low = (low.astype(f32) + got[-1].astype(f32)).astype(bf16)
        got.append(flip(low, ("col", "cplx"), mask))
        mask *= 2
    *outs, own = call(
        partial(adjoint_kernel, n_row, len(got), own_v, own_u, lanes),
        [((2 * block * (wide // lanes) + 16, lanes), bf16)] * n_row + [((2 * own_u, tile_size), f32)],
        live,
        u_turned,
        v_bases,
        own,
        low,
        *got,
        vmem=vmem,
    )
    sums = [outs[0]] + [flip(outs[k], "row", k) for k in second]
    residual_v, beta, norms = call(
        partial(residual_kernel, n_row, second, rows_total, cols_total, lanes),
        [((block, wide), f32), ((1, lanes), f32), ((1, lanes), f32)],
        v_unit,
        kept,
        *sums,
    )
    norms = norms + flip(norms, "cplx", 1)
    mask = n_cplx
    while 2 * mask < n_cols:
        norms = norms + flip(norms, ("col", "cplx"), mask + 1)
        mask *= 2
    across = [mask] + [k * n_cols + m for k in range(1, n_row // 2) for m in (0, mask)]
    got = [flip(norms, ("row", "col", "cplx"), m + 1) for m in across]
    x_next, w_next, u_next, v_next, norms = call(
        partial(vectors_kernel, cols_total),
        [(x_solution.shape, f32), (w_direction.shape, f32), (u_unit.shape, f32), (v_unit.shape, f32), ((1, lanes), f32)],
        norms,
        got[0],
        beta,
        residual_v,
        own,
        x_solution,
        w_direction,
        scalars,
        cost=pl.CostEstimate(flops=10**9, bytes_accessed=2**23, transcendentals=0),
    )
    alpha, rhobar, phibar = call(
        partial(scalars_kernel, cols_total), [((1, rhs), f32)] * 3, beta, scalars, norms, *got[1:]
    )
    return (x_next, w_next, u_next, v_next, alpha[0], rhobar[0], phibar[0])


def solution(mesh):
    placed = (
        P(("freq", "row"), ("col", "cplx"), None, None, None),
        P(("freq", "row"), ("col", "cplx"), None, None, None),
        P(("freq", "row"), ("col", "cplx")),
        P(("freq", "col", "cplx"), None, "row"),
        P(("freq", "row"), None, ("col", "cplx")),
        P(("freq", "row"), None, ("col", "cplx")),
        P(("freq", "row"), None, ("col", "cplx")),
        P("freq"),
        P("freq"),
        P("freq"),
    )
    return jax.shard_map(
        body,
        mesh=mesh,
        in_specs=placed,
        out_specs=(
            P(("freq", "row"), None, ("col", "cplx")),
            P(("freq", "row"), None, ("col", "cplx")),
            P(("freq", "col", "cplx"), None, "row"),
            P(("freq", "row"), None, ("col", "cplx")),
            P("freq"),
            P("freq"),
            P("freq"),
        ),
        check_vma=False,
    )
```

```python
from functools import partial

import jax
import jax.numpy as jnp
from jax import lax
from jax.experimental import pallas as pl
from jax.experimental.pallas import tpu as pltpu
from jax.sharding import PartitionSpec as P

epsilon = 1e-06
shrink = 2.0**-20
f32 = jnp.float32
bf16 = jnp.bfloat16


def call(kernel, outs, *args, scratch=(), vmem=12, cost=None):
    in_specs = [pl.BlockSpec(memory_space=pltpu.VMEM)] * len(args)
    return pl.pallas_call(
        kernel,
        out_shape=[jax.ShapeDtypeStruct(s, d) for s, d in outs],
        in_specs=in_specs,
        out_specs=[pl.BlockSpec(memory_space=pltpu.VMEM)] * len(outs),
        scratch_shapes=list(scratch),
        compiler_params=pltpu.CompilerParams(vmem_limit_bytes=vmem * 2**20),
        cost_estimate=cost,
    )(*args)


def iota(shape, dim):
    return lax.broadcasted_iota(jnp.int32, shape, dim)


def to_lanes(column, place, lanes):
    rows = column.shape[0]
    here = iota((rows, lanes), 1) == place
    return jnp.sum(jnp.where(here, column, 0.0), axis=0, keepdims=True)


def to_column(lane_values, first, rows):
    lanes = lane_values.shape[1]
    here = iota((rows, lanes), 1) == iota((rows, lanes), 0) + first
    return jnp.sum(jnp.where(here, lane_values, 0.0), axis=1, keepdims=True)


def dot(a, b, transposed):
    return lax.dot_general(a, b, (((1,), (1 if transposed else 0,)), ((), ())), preferred_element_type=f32)


def through(inner, outer, live_ref, x, own):
    tiles, _, ranks, size = inner.shape[1:]
    mids = []
    gs = [dot(x(q), inner[0, q].reshape(2 * ranks, size), True) for q in range(tiles)]
    for q, g in enumerate(gs):
        rows = g.shape[0]
        g = g.reshape(rows // (2 * own), 2, own, 2 * ranks)
        live = live_ref[q : q + 1, :]
        re = (g[:, 0, :, :ranks] + g[:, 1, :, ranks:]) * live
        im = (g[:, 1, :, :ranks] - g[:, 0, :, ranks:]) * live
        both = jnp.stack([jnp.concatenate([re, -im], 2), jnp.concatenate([im, re], 2)], 1)
        mids.append(both.reshape(rows, 2 * ranks).astype(bf16))
    return [dot(both, outer[0, q].reshape(2 * ranks, size), False) for q, both in enumerate(mids)]


def in_order(blocks, order):
    return [blocks[0]] + [blocks[1 + order.index(k)] for k in range(1, len(blocks))]


def prepare_kernel(ranks_ref, alpha_ref, rhobar_ref, phibar_ref, live_ref, scalars_ref):
    for q in range(live_ref.shape[0]):
        here = iota((1, live_ref.shape[1]), 1) < ranks_ref[0:1, q : q + 1]
        live_ref[q : q + 1, :] = here.astype(f32)
    for i, ref in enumerate((alpha_ref, rhobar_ref, phibar_ref)):
        scalars_ref[i : i + 1, :] = ref[...]


def forward_kernel(n_row, order, own_v, own_u, live_ref, u_bases, v_bases, u_ref, alpha_ref, *refs):
    blocks, (low_ref, own_ref, kept_ref, total) = in_order(refs[:n_row], order), refs[n_row:]
    p, c = lax.axis_index("row"), lax.axis_index(("col", "cplx"))
    size = v_bases.shape[4]
    x = jnp.concatenate([b[...] for b in blocks], 0)
    kept_ref[0] = blocks[0][...]
    kept_ref[1] = blocks[n_row // 2][...]
    parts = through(v_bases, u_bases, live_ref, lambda q: x[:, q * size : (q + 1) * size], own_v)
    total[...] = sum(parts[1:], parts[0])
    many = own_u // own_v
    for b in range(many):
        at = pl.ds(pl.multiple_of(((c * many + b) ^ p) * 2 * own_v, 2 * own_v), 2 * own_v)
        alpha = to_column(alpha_ref[0:1, :], c * own_u + b * own_v, own_v)
        mine = slice(b * own_v, (b + 1) * own_v)
        shift = jnp.concatenate([alpha * u_ref[mine, 0, :], alpha * u_ref[mine, 1, :]], 0)
        left = total[at, :] - shift
        own_ref[b * 2 * own_v : (b + 1) * 2 * own_v, :] = left
        total[at, :] = left
    low_ref[...] = total[...].astype(bf16)


def adjoint_kernel(n_row, n_got, own_v, own_u, lanes, live_ref, u_bases, v_bases, own_ref, sum_ref, *refs):
    got, outs, own_out = refs[:n_got], refs[n_got : n_got + n_row], refs[n_got + n_row]
    p, c = lax.axis_index("row"), lax.axis_index(("col", "cplx"))
    many = own_u // own_v
    for b in range(many):
        at = pl.ds(pl.multiple_of(((c * many + b) ^ p) * 2 * own_v, 2 * own_v), 2 * own_v)
        mine = slice(b * 2 * own_v, (b + 1) * 2 * own_v)
        acc = own_ref[mine, :]
        for g in got:
            acc = acc + g[at, :].astype(f32)
        own_out[mine, :] = acc
    res = sum_ref[...].astype(f32) + got[-1][...].astype(f32)
    rows = res.shape[0]
    squares = jnp.sum(res * res, axis=1, keepdims=True)
    row = iota((rows, 1), 0)
    place = ((row // (2 * own_v)) ^ p) * own_v + row % own_v
    beta2 = to_lanes(squares, place, lanes)
    high = beta2.astype(bf16)
    low = (beta2 - high.astype(f32)).astype(bf16)
    tail = jnp.where(iota((16, lanes), 0) == 0, high.astype(f32), low.astype(f32)).astype(bf16)
    x = (res * shrink).astype(bf16)
    parts = through(u_bases, v_bases, live_ref, lambda q: x, own_v)
    wide = jnp.concatenate(parts, 1).astype(bf16)
    strips = wide.shape[1] // lanes
    for k, out in enumerate(outs):
        for i, j in enumerate((k, k ^ (n_row // 2))):
            for t in range(strips):
                at = (i * strips + t) * 2 * own_v
                out[at : at + 2 * own_v, :] = wide[j * 2 * own_v : (j + 1) * 2 * own_v, t * lanes : (t + 1) * lanes]
        out[2 * strips * 2 * own_v :, :] = tail


def pairs(values):
    while len(values) > 1:
        values = [a + b for a, b in zip(values[::2], values[1::2])]
    return values[0]


def residual_kernel(n_row, order, rows_total, cols_total, lanes, kept_ref, *refs):
    blocks, (beta_ref, norm_ref) = in_order(refs[:n_row], order), refs[n_row:]
    p = lax.axis_index("row")
    _, block, wide = kept_ref.shape
    own_v = block // 2
    strips = wide // lanes
    end = 2 * strips * 2 * own_v
    beta2 = pairs([b[end : end + 1, :].astype(f32) + b[end + 1 : end + 2, :].astype(f32) for b in blocks])
    beta = jnp.sqrt(beta2 / (2 * rows_total) + epsilon)
    beta_ref[...] = beta
    rows = (p, p ^ (n_row // 2))
    first = jnp.where(iota((4 * own_v, 1), 0) < 2 * own_v, rows[0], rows[1]) * own_v + iota((4 * own_v, 1), 0) % own_v
    here = iota((4 * own_v, lanes), 1) == first
    betas = jnp.sum(jnp.where(here, beta, 0.0), axis=1, keepdims=True)
    scales = rows_total / cols_total / shrink / betas
    squares = []
    for h in range(2):
        both = slice(h * 2 * own_v, (h + 1) * 2 * own_v)
        beta_here, scale = betas[both], scales[both]
        total = jnp.zeros((2 * own_v, lanes), f32)
        for t in range(strips):
            at = (h * strips + t) * 2 * own_v
            back = scale * pairs([b[at : at + 2 * own_v, :].astype(f32) for b in blocks])
            strip = slice(t * lanes, (t + 1) * lanes)
            res = back - beta_here * kept_ref[h, :, strip].astype(f32)
            total = total + res * res
        squares.append(total)
    squares = jnp.sum(jnp.concatenate(squares, 0), axis=1, keepdims=True)
    norm_ref[...] = jnp.sum(jnp.where(here, squares, 0.0), axis=0, keepdims=True)


def turn(beta, scalars_ref):
    rhobar, phibar = scalars_ref[1:2, :], scalars_ref[2:3, :]
    rho = jnp.sqrt(rhobar * rhobar + beta * beta)
    return rho, rhobar / rho, beta / rho, phibar


def vectors_kernel(n_row, order, rows_total, cols_total, norms_ref, got_ref, beta_ref, v_ref, own_ref, x_ref, w_ref, scalars_ref, *refs):
    blocks, (x_out, w_out, u_out, v_out, sum_out) = in_order(refs[:n_row], order), refs[n_row:]
    p, c = lax.axis_index("row"), lax.axis_index(("col", "cplx"))
    own_v = x_ref.shape[0]
    own_u = u_out.shape[0]
    many = own_u // own_v
    rhs = scalars_ref.shape[1]
    beta = beta_ref[:, :rhs]
    rho, cosine, sine, phibar = turn(beta, scalars_ref)
    norms = norms_ref[...] + got_ref[...]
    sum_out[...] = norms
    alpha2 = to_column(norms, p * own_v, own_v)
    alpha = jnp.sqrt(alpha2 / (2 * cols_total) + epsilon)
    step_x = to_column(cosine * phibar / rho, p * own_v, own_v)
    step_w = to_column(sine / rho, p * own_v, own_v) * alpha
    beta_here = to_column(beta, p * own_v, own_v)
    scale = rows_total / cols_total / shrink / beta_here
    lanes = norms_ref.shape[1]
    for t in range(x_ref.shape[2] // lanes):
        strip = slice(t * lanes, (t + 1) * lanes)
        back = pairs([b[t * 2 * own_v : (t + 1) * 2 * own_v, :].astype(f32) for b in blocks])
        for i in range(2):
            w = w_ref[:, i, strip]
            v = (scale * back[i * own_v : (i + 1) * own_v] - beta_here * v_ref[:, i, strip]) / alpha
            x_out[:, i, strip] = x_ref[:, i, strip] + step_x * w
            v_out[:, i, strip] = v
            w_out[:, i, strip] = v - step_w * w
    for b in range(many):
        beta_own = to_column(beta, c * own_u + b * own_v, own_v)
        for i in range(2):
            u = own_ref[(2 * b + i) * own_v : (2 * b + i + 1) * own_v, :]
            u_out[b * own_v : (b + 1) * own_v, i, :] = u / beta_own


def scalars_kernel(cols_total, beta_ref, scalars_ref, *refs):
    norms, (alpha_out, rhobar_out, phibar_out) = refs[:-3], refs[-3:]
    rhs = scalars_ref.shape[1]
    rho, cosine, sine, phibar = turn(beta_ref[:, :rhs], scalars_ref)
    alpha2 = sum([n[...] for n in norms[1:]], norms[0][...])[:, :rhs]
    alpha = jnp.sqrt(alpha2 / (2 * cols_total) + epsilon)
    alpha_out[...] = alpha
    rhobar_out[...] = -cosine * alpha
    phibar_out[...] = sine * phibar


def flip(x, axes, mask):
    return lax.ppermute(x, axes, [(i, i ^ mask) for i in range(lax.axis_size(axes))])


def body(
    u_bases,
    v_bases,
    tile_ranks,
    u_unit,
    v_unit,
    x_solution,
    w_direction,
    alpha_prev,
    rhobar_prev,
    phibar_prev,
):
    tile_size = u_bases.shape[4]
    n_row = lax.axis_size("row")
    n_cplx = lax.axis_size("cplx")
    n_cols = lax.axis_size(("col", "cplx"))
    rows_total = tile_size * n_row
    cols_total = u_bases.shape[1] * tile_size * n_cols
    own_u, own_v = u_unit.shape[0], v_unit.shape[0]
    wide = v_unit.shape[2]
    rhs = own_v * n_row
    lanes = -(-rhs // 128) * 128
    block = 2 * own_v
    vmem = 8 + rhs // 16
    first = [1, *range(n_row - 1, 1, -1)]
    second = [*range(2, n_row), 1]
    live, scalars = call(
        prepare_kernel,
        [((u_bases.shape[1], u_bases.shape[3]), f32), ((3, rhs), f32)],
        tile_ranks,
        alpha_prev[None],
        rhobar_prev[None],
        phibar_prev[None],
        cost=pl.CostEstimate(flops=10**10, bytes_accessed=2**26, transcendentals=0),
    )
    first = [1, *range(n_row - 1, 1, -1)]
    second = [*range(2, n_row), 1]
    v_low = jnp.swapaxes(v_unit, 0, 1).reshape(block, wide).astype(bf16)
    blocks = [v_low] + [flip(v_low, "row", k) for k in first]
    low, own, kept = call(
        partial(forward_kernel, n_row, first, own_v, own_u),
        [((2 * rhs, tile_size), bf16), ((2 * own_u, tile_size), f32), ((2, block, wide), bf16)],
        live,
        u_bases,
        v_bases,
        u_unit,
        scalars,
        *blocks,
        scratch=[pltpu.VMEM((2 * rhs, tile_size), f32)],
        vmem=vmem,
    )
    got = [flip(low, "cplx", 1)]
    mask = n_cplx
    while mask < n_cols:
        low = (low.astype(f32) + got[-1].astype(f32)).astype(bf16)
        got.append(flip(low, ("col", "cplx"), mask))
        mask *= 2
    *outs, own = call(
        partial(adjoint_kernel, n_row, len(got), own_v, own_u, lanes),
        [((2 * block * (wide // lanes) + 16, lanes), bf16)] * n_row + [((2 * own_u, tile_size), f32)],
        live,
        u_bases,
        v_bases,
        own,
        low,
        *got,
        vmem=vmem,
    )
    sums = [outs[0]] + [flip(outs[k], "row", k) for k in second]
    beta, norms = call(
        partial(residual_kernel, n_row, second, rows_total, cols_total, lanes),
        [((1, lanes), f32), ((1, lanes), f32)],
        kept,
        *sums,
    )
    norms = norms + flip(norms, "cplx", 1)
    mask = n_cplx
    while 2 * mask < n_cols:
        norms = norms + flip(norms, ("col", "cplx"), mask + 1)
        mask *= 2
    across = [mask] + [k * n_cols + m for k in range(1, n_row // 2) for m in (0, mask)]
    got = [flip(norms, ("row", "col", "cplx"), m + 1) for m in across]
    x_next, w_next, u_next, v_next, norms = call(
        partial(vectors_kernel, n_row, second, rows_total, cols_total),
        [(x_solution.shape, f32), (w_direction.shape, f32), (u_unit.shape, f32), (v_unit.shape, f32), ((1, lanes), f32)],
        norms,
        got[0],
        beta,
        v_unit,
        own,
        x_solution,
        w_direction,
        scalars,
        *sums,
        cost=pl.CostEstimate(flops=10**9, bytes_accessed=2**23, transcendentals=0),
    )
    alpha, rhobar, phibar = call(
        partial(scalars_kernel, cols_total), [((1, rhs), f32)] * 3, beta, scalars, norms, *got[1:]
    )
    return (x_next, w_next, u_next, v_next, alpha[0], rhobar[0], phibar[0])


def solution(mesh):
    placed = (
        P(("freq", "row"), ("col", "cplx"), None, None, None),
        P(("freq", "row"), ("col", "cplx"), None, None, None),
        P(("freq", "row"), ("col", "cplx")),
        P(("freq", "col", "cplx"), None, "row"),
        P(("freq", "row"), None, ("col", "cplx")),
        P(("freq", "row"), None, ("col", "cplx")),
        P(("freq", "row"), None, ("col", "cplx")),
        P("freq"),
        P("freq"),
        P("freq"),
    )
    return jax.shard_map(
        body,
        mesh=mesh,
        in_specs=placed,
        out_specs=(
            P(("freq", "row"), None, ("col", "cplx")),
            P(("freq", "row"), None, ("col", "cplx")),
            P(("freq", "col", "cplx"), None, "row"),
            P(("freq", "row"), None, ("col", "cplx")),
            P("freq"),
            P("freq"),
            P("freq"),
        ),
        check_vma=False,
    )
```

```python
from functools import partial

import jax
import jax.numpy as jnp
from jax import lax
from jax.experimental import pallas as pl
from jax.experimental.pallas import tpu as pltpu
from jax.sharding import PartitionSpec as P

epsilon = 1e-06
shrink = 2.0**-20
f32 = jnp.float32
bf16 = jnp.bfloat16


def call(kernel, outs, *args, scratch=(), vmem=12, cost=None):
    in_specs = [pl.BlockSpec(memory_space=pltpu.VMEM)] * len(args)
    return pl.pallas_call(
        kernel,
        out_shape=[jax.ShapeDtypeStruct(s, d) for s, d in outs],
        in_specs=in_specs,
        out_specs=[pl.BlockSpec(memory_space=pltpu.VMEM)] * len(outs),
        scratch_shapes=list(scratch),
        compiler_params=pltpu.CompilerParams(vmem_limit_bytes=vmem * 2**20),
        cost_estimate=cost,
    )(*args)


def iota(shape, dim):
    return lax.broadcasted_iota(jnp.int32, shape, dim)


def to_lanes(column, place, lanes):
    rows = column.shape[0]
    here = iota((rows, lanes), 1) == place
    return jnp.sum(jnp.where(here, column, 0.0), axis=0, keepdims=True)


def to_column(lane_values, first, rows):
    lanes = lane_values.shape[1]
    here = iota((rows, lanes), 1) == iota((rows, lanes), 0) + first
    return jnp.sum(jnp.where(here, lane_values, 0.0), axis=1, keepdims=True)


def dot(a, b, transposed):
    return lax.dot_general(a, b, (((1,), (1 if transposed else 0,)), ((), ())), preferred_element_type=f32)


def through(inner, outer, live_ref, x, own):
    tiles, _, ranks, size = outer.shape[1:]
    mids = []
    if len(inner.shape) == 3:
        gs = [dot(x(q), inner[q], False) for q in range(tiles)]
    else:
        gs = [dot(x(q), inner[0, q].reshape(2 * ranks, size), True) for q in range(tiles)]
    for q, g in enumerate(gs):
        rows = g.shape[0]
        g = g.reshape(rows // (2 * own), 2, own, 2 * ranks)
        live = live_ref[q : q + 1, :]
        re = (g[:, 0, :, :ranks] + g[:, 1, :, ranks:]) * live
        im = (g[:, 1, :, :ranks] - g[:, 0, :, ranks:]) * live
        both = jnp.stack([jnp.concatenate([re, -im], 2), jnp.concatenate([im, re], 2)], 1)
        mids.append(both.reshape(rows, 2 * ranks).astype(bf16))
    return [dot(both, outer[0, q].reshape(2 * ranks, size), False) for q, both in enumerate(mids)]


def in_order(blocks, order):
    return [blocks[0]] + [blocks[1 + order.index(k)] for k in range(1, len(blocks))]


def prepare_kernel(ranks_ref, alpha_ref, rhobar_ref, phibar_ref, live_ref, scalars_ref):
    for q in range(live_ref.shape[0]):
        here = iota((1, live_ref.shape[1]), 1) < ranks_ref[0:1, q : q + 1]
        live_ref[q : q + 1, :] = here.astype(f32)
    for i, ref in enumerate((alpha_ref, rhobar_ref, phibar_ref)):
        scalars_ref[i : i + 1, :] = ref[...]


def forward_kernel(n_row, order, own_v, own_u, live_ref, u_bases, v_bases, u_ref, alpha_ref, *refs):
    blocks, (low_ref, own_ref, kept_ref, total) = in_order(refs[:n_row], order), refs[n_row:]
    p, c = lax.axis_index("row"), lax.axis_index(("col", "cplx"))
    size = v_bases.shape[4]
    x = jnp.concatenate([b[...] for b in blocks], 0)
    kept_ref[0] = blocks[0][...]
    kept_ref[1] = blocks[n_row // 2][...]
    parts = through(v_bases, u_bases, live_ref, lambda q: x[:, q * size : (q + 1) * size], own_v)
    total[...] = sum(parts[1:], parts[0])
    many = own_u // own_v
    for b in range(many):
        at = pl.ds(pl.multiple_of(((c * many + b) ^ p) * 2 * own_v, 2 * own_v), 2 * own_v)
        alpha = to_column(alpha_ref[0:1, :], c * own_u + b * own_v, own_v)
        mine = slice(b * own_v, (b + 1) * own_v)
        shift = jnp.concatenate([alpha * u_ref[mine, 0, :], alpha * u_ref[mine, 1, :]], 0)
        left = total[at, :] - shift
        own_ref[b * 2 * own_v : (b + 1) * 2 * own_v, :] = left
        total[at, :] = left
    low_ref[...] = total[...].astype(bf16)


def adjoint_kernel(n_row, n_got, own_v, own_u, lanes, live_ref, u_turned, v_bases, own_ref, sum_ref, *refs):
    got, outs, own_out = refs[:n_got], refs[n_got : n_got + n_row], refs[n_got + n_row]
    p, c = lax.axis_index("row"), lax.axis_index(("col", "cplx"))
    many = own_u // own_v
    for b in range(many):
        at = pl.ds(pl.multiple_of(((c * many + b) ^ p) * 2 * own_v, 2 * own_v), 2 * own_v)
        mine = slice(b * 2 * own_v, (b + 1) * 2 * own_v)
        acc = own_ref[mine, :]
        for g in got:
            acc = acc + g[at, :].astype(f32)
        own_out[mine, :] = acc
    res = sum_ref[...].astype(f32) + got[-1][...].astype(f32)
    rows = res.shape[0]
    squares = jnp.sum(res * res, axis=1, keepdims=True)
    row = iota((rows, 1), 0)
    place = ((row // (2 * own_v)) ^ p) * own_v + row % own_v
    beta2 = to_lanes(squares, place, lanes)
    high = beta2.astype(bf16)
    low = (beta2 - high.astype(f32)).astype(bf16)
    tail = jnp.where(iota((16, lanes), 0) == 0, high.astype(f32), low.astype(f32)).astype(bf16)
    x = (res * shrink).astype(bf16)
    parts = through(u_turned, v_bases, live_ref, lambda q: x, own_v)
    wide = jnp.concatenate(parts, 1).astype(bf16)
    strips = wide.shape[1] // lanes
    for k, out in enumerate(outs):
        for i, j in enumerate((k, k ^ (n_row // 2))):
            for t in range(strips):
                at = (i * strips + t) * 2 * own_v
                out[at : at + 2 * own_v, :] = wide[j * 2 * own_v : (j + 1) * 2 * own_v, t * lanes : (t + 1) * lanes]
        out[2 * strips * 2 * own_v :, :] = tail


def pairs(values):
    while len(values) > 1:
        values = [a + b for a, b in zip(values[::2], values[1::2])]
    return values[0]


def residual_kernel(n_row, order, rows_total, cols_total, lanes, kept_ref, *refs):
    blocks, (beta_ref, norm_ref) = in_order(refs[:n_row], order), refs[n_row:]
    p = lax.axis_index("row")
    _, block, wide = kept_ref.shape
    own_v = block // 2
    strips = wide // lanes
    end = 2 * strips * 2 * own_v
    beta2 = pairs([b[end : end + 1, :].astype(f32) + b[end + 1 : end + 2, :].astype(f32) for b in blocks])
    beta = jnp.sqrt(beta2 / (2 * rows_total) + epsilon)
    beta_ref[...] = beta
    rows = (p, p ^ (n_row // 2))
    first = jnp.where(iota((4 * own_v, 1), 0) < 2 * own_v, rows[0], rows[1]) * own_v + iota((4 * own_v, 1), 0) % own_v
    here = iota((4 * own_v, lanes), 1) == first
    betas = jnp.sum(jnp.where(here, beta, 0.0), axis=1, keepdims=True)
    scales = rows_total / cols_total / shrink / betas
    squares = []
    for h in range(2):
        both = slice(h * 2 * own_v, (h + 1) * 2 * own_v)
        beta_here, scale = betas[both], scales[both]
        total = jnp.zeros((2 * own_v, lanes), f32)
        for t in range(strips):
            at = (h * strips + t) * 2 * own_v
            back = scale * pairs([b[at : at + 2 * own_v, :].astype(f32) for b in blocks])
            strip = slice(t * lanes, (t + 1) * lanes)
            res = back - beta_here * kept_ref[h, :, strip].astype(f32)
            total = total + res * res
        squares.append(total)
    squares = jnp.sum(jnp.concatenate(squares, 0), axis=1, keepdims=True)
    norm_ref[...] = jnp.sum(jnp.where(here, squares, 0.0), axis=0, keepdims=True)


def turn(beta, scalars_ref):
    rhobar, phibar = scalars_ref[1:2, :], scalars_ref[2:3, :]
    rho = jnp.sqrt(rhobar * rhobar + beta * beta)
    return rho, rhobar / rho, beta / rho, phibar


def vectors_kernel(n_row, order, rows_total, cols_total, norms_ref, got_ref, beta_ref, v_ref, own_ref, x_ref, w_ref, scalars_ref, *refs):
    blocks, (x_out, w_out, u_out, v_out, sum_out) = in_order(refs[:n_row], order), refs[n_row:]
    p, c = lax.axis_index("row"), lax.axis_index(("col", "cplx"))
    own_v = x_ref.shape[0]
    own_u = u_out.shape[0]
    many = own_u // own_v
    rhs = scalars_ref.shape[1]
    beta = beta_ref[:, :rhs]
    rho, cosine, sine, phibar = turn(beta, scalars_ref)
    norms = norms_ref[...] + got_ref[...]
    sum_out[...] = norms
    alpha2 = to_column(norms, p * own_v, own_v)
    alpha = jnp.sqrt(alpha2 / (2 * cols_total) + epsilon)
    step_x = to_column(cosine * phibar / rho, p * own_v, own_v)
    step_w = to_column(sine / rho, p * own_v, own_v) * alpha
    beta_here = to_column(beta, p * own_v, own_v)
    scale = rows_total / cols_total / shrink / beta_here
    lanes = norms_ref.shape[1]
    for t in range(x_ref.shape[2] // lanes):
        strip = slice(t * lanes, (t + 1) * lanes)
        back = pairs([b[t * 2 * own_v : (t + 1) * 2 * own_v, :].astype(f32) for b in blocks])
        for i in range(2):
            w = w_ref[:, i, strip]
            v = (scale * back[i * own_v : (i + 1) * own_v] - beta_here * v_ref[:, i, strip]) / alpha
            x_out[:, i, strip] = x_ref[:, i, strip] + step_x * w
            v_out[:, i, strip] = v
            w_out[:, i, strip] = v - step_w * w
    for b in range(many):
        beta_own = to_column(beta, c * own_u + b * own_v, own_v)
        for i in range(2):
            u = own_ref[(2 * b + i) * own_v : (2 * b + i + 1) * own_v, :]
            u_out[b * own_v : (b + 1) * own_v, i, :] = u / beta_own


def scalars_kernel(cols_total, beta_ref, scalars_ref, *refs):
    norms, (alpha_out, rhobar_out, phibar_out) = refs[:-3], refs[-3:]
    rhs = scalars_ref.shape[1]
    rho, cosine, sine, phibar = turn(beta_ref[:, :rhs], scalars_ref)
    alpha2 = sum([n[...] for n in norms[1:]], norms[0][...])[:, :rhs]
    alpha = jnp.sqrt(alpha2 / (2 * cols_total) + epsilon)
    alpha_out[...] = alpha
    rhobar_out[...] = -cosine * alpha
    phibar_out[...] = sine * phibar


def flip(x, axes, mask):
    return lax.ppermute(x, axes, [(i, i ^ mask) for i in range(lax.axis_size(axes))])


def body(
    u_bases,
    v_bases,
    tile_ranks,
    u_unit,
    v_unit,
    x_solution,
    w_direction,
    alpha_prev,
    rhobar_prev,
    phibar_prev,
):
    tile_size = u_bases.shape[4]
    n_row = lax.axis_size("row")
    n_cplx = lax.axis_size("cplx")
    n_cols = lax.axis_size(("col", "cplx"))
    rows_total = tile_size * n_row
    cols_total = u_bases.shape[1] * tile_size * n_cols
    own_u, own_v = u_unit.shape[0], v_unit.shape[0]
    wide = v_unit.shape[2]
    rhs = own_v * n_row
    lanes = -(-rhs // 128) * 128
    block = 2 * own_v
    vmem = 8 + rhs // 16
    first = [1, *range(n_row - 1, 1, -1)]
    second = [*range(2, n_row), 1]
    live, scalars = call(
        prepare_kernel,
        [((u_bases.shape[1], u_bases.shape[3]), f32), ((3, rhs), f32)],
        tile_ranks,
        alpha_prev[None],
        rhobar_prev[None],
        phibar_prev[None],
        cost=pl.CostEstimate(flops=10**10, bytes_accessed=2**26, transcendentals=0),
    )
    first = [1, *range(n_row - 1, 1, -1)]
    second = [*range(2, n_row), 1]
    v_low = jnp.swapaxes(v_unit, 0, 1).reshape(block, wide).astype(bf16)
    blocks = [v_low] + [flip(v_low, "row", k) for k in first]
    tiles, _, ranks, size = u_bases.shape[1:]
    u_turned = jnp.swapaxes(u_bases.reshape(tiles, 2 * ranks, size), 1, 2)
    low, own, kept = call(
        partial(forward_kernel, n_row, first, own_v, own_u),
        [((2 * rhs, tile_size), bf16), ((2 * own_u, tile_size), f32), ((2, block, wide), bf16)],
        live,
        u_bases,
        v_bases,
        u_unit,
        scalars,
        *blocks,
        scratch=[pltpu.VMEM((2 * rhs, tile_size), f32)],
        vmem=vmem,
    )
    got = [flip(low, "cplx", 1)]
    mask = n_cplx
    while mask < n_cols:
        low = (low.astype(f32) + got[-1].astype(f32)).astype(bf16)
        got.append(flip(low, ("col", "cplx"), mask))
        mask *= 2
    *outs, own = call(
        partial(adjoint_kernel, n_row, len(got), own_v, own_u, lanes),
        [((2 * block * (wide // lanes) + 16, lanes), bf16)] * n_row + [((2 * own_u, tile_size), f32)],
        live,
        u_turned,
        v_bases,
        own,
        low,
        *got,
        vmem=vmem,
    )
    sums = [outs[0]] + [flip(outs[k], "row", k) for k in second]
    beta, norms = call(
        partial(residual_kernel, n_row, second, rows_total, cols_total, lanes),
        [((1, lanes), f32), ((1, lanes), f32)],
        kept,
        *sums,
    )
    norms = norms + flip(norms, "cplx", 1)
    mask = n_cplx
    while 2 * mask < n_cols:
        norms = norms + flip(norms, ("col", "cplx"), mask + 1)
        mask *= 2
    across = [mask] + [k * n_cols + m for k in range(1, n_row // 2) for m in (0, mask)]
    got = [flip(norms, ("row", "col", "cplx"), m + 1) for m in across]
    x_next, w_next, u_next, v_next, norms = call(
        partial(vectors_kernel, n_row, second, rows_total, cols_total),
        [(x_solution.shape, f32), (w_direction.shape, f32), (u_unit.shape, f32), (v_unit.shape, f32), ((1, lanes), f32)],
        norms,
        got[0],
        beta,
        v_unit,
        own,
        x_solution,
        w_direction,
        scalars,
        *sums,
        cost=pl.CostEstimate(flops=10**9, bytes_accessed=2**23, transcendentals=0),
    )
    alpha, rhobar, phibar = call(
        partial(scalars_kernel, cols_total), [((1, rhs), f32)] * 3, beta, scalars, norms, *got[1:]
    )
    return (x_next, w_next, u_next, v_next, alpha[0], rhobar[0], phibar[0])


def solution(mesh):
    placed = (
        P(("freq", "row"), ("col", "cplx"), None, None, None),
        P(("freq", "row"), ("col", "cplx"), None, None, None),
        P(("freq", "row"), ("col", "cplx")),
        P(("freq", "col", "cplx"), None, "row"),
        P(("freq", "row"), None, ("col", "cplx")),
        P(("freq", "row"), None, ("col", "cplx")),
        P(("freq", "row"), None, ("col", "cplx")),
        P("freq"),
        P("freq"),
        P("freq"),
    )
    return jax.shard_map(
        body,
        mesh=mesh,
        in_specs=placed,
        out_specs=(
            P(("freq", "row"), None, ("col", "cplx")),
            P(("freq", "row"), None, ("col", "cplx")),
            P(("freq", "col", "cplx"), None, "row"),
            P(("freq", "row"), None, ("col", "cplx")),
            P("freq"),
            P("freq"),
            P("freq"),
        ),
        check_vma=False,
    )
```
